128 devices in a mesh: section: 8 (over x, core), expert: 16 (over y, z).
Axes of the slice: x: 4, y: 4, z: 4, core: 2. Of those that a mesh axis runs over, the one named last changes fastest.
Arguments:
- inputs: bfloat16 [8, 2048, 2048], P('section', 'expert'), may hold values from -6 to 6
- out_grad: bfloat16 [8, 2048, 2048], P('section', 'expert'), may hold values from -6 to 6
- expert_ids: int32 [8, 2048, 8], P('section', 'expert'), may hold values from 0 to 15, all different within a row; in each aligned block of 128 rows (0 to 127, 128 to 255, ..., all dimensions but the last counted through in order) at most 72 rows name the same one
- gate_probs: bfloat16 [8, 2048, 8], P('section', 'expert'), may hold values from 0.049804688 to 0.59765625
- gate_weight: bfloat16 [8, 16, 2048, 768], P('section', 'expert'), may hold values from -0.125 to 0.125
- up_weight: bfloat16 [8, 16, 2048, 768], P('section', 'expert'), may hold values from -0.125 to 0.125
- down_weight: bfloat16 [8, 16, 768, 2048], P('section', 'expert'), may hold values from -0.21875 to 0.21875
Outputs:
- handed_grad: bfloat16 [8, 2048, 2048], P('section', 'expert')
- gate_grad: bfloat16 [8, 2048, 8], P('section', 'expert')
- gate_wgrad: bfloat16 [8, 16, 2048, 768], P('section', 'expert')
- up_wgrad: bfloat16 [8, 16, 2048, 768], P('section', 'expert')
- down_wgrad: bfloat16 [8, 16, 768, 2048], P('section', 'expert')
The draws below stay inside these ranges and needn't reach their ends.
Inputs may be any that keep to these rules, and one draw needn't show every extreme that they name: `expert_ids`: each row names 8 different experts. Among the rows of one device (aligned blocks of 128 rows) no expert is named by more than 72 rows, a bound that some block reaches.
All inputs are finite; a program needn't handle non-finite values.
Results may differ from the reference program's by a relative error of at most 0.011.
Values may be sent and summed in bfloat16 or wider, within the bound.
No kernel may reach another device: no remote copies, remote signals or barrier semaphores. Data moves between devices by JAX's collectives and lax.ppermute only.
A program may use at most 128 MiB of HBM per device.

```python
import math
import jax
import jax.numpy as jnp
import numpy as np
from jax import lax

D = 2048
FF = 768
TOPK = 8
TOK_DEV = 128
EXPERTS = 16
CAP = 72
TOKENS = 2048
N_SECTION = 8
N_EXPERT = 16


def steps_of(key, extent, split, low, high):
    loudness, own = 1.0, jax.random.fold_in(key, 6)
    for dim, parts in split:
        heights = jnp.exp(jax.random.uniform(jax.random.fold_in(own, dim), (parts,), jnp.float32, low / len(split), high / len(split)))
        loudness = loudness * jnp.repeat(heights, extent[dim] // parts).reshape([-1 if axis == dim else 1 for axis in range(len(extent))])
    return loudness


def deal_out(key, own, number, rows, count, top, reach, skew):
    sequence = jax.random.permutation(key, count)
    packed, ordinary = load_shares(count, rows * top, reach, skew, True), load_shares(count, rows * top, reach, skew, False)
    places = jnp.arange(count)

    def named(lengths, turn):
        used = int((lengths > 0).sum())
        fixed = max(1, used // 4)
        moved = fixed + (places - fixed + turn * (used - fixed)) % max(1, count - fixed)
        return jnp.zeros((count,), jnp.int32).at[sequence[jnp.where(places < fixed, places, moved)]].set(jnp.asarray(lengths, jnp.int32))

    lengths = jnp.where(number % 4 == 0, named(packed, number // 4), named(ordinary, number - number // 4 - 1))
    mixed = jax.random.permutation(jax.random.fold_in(own, 3), count)
    donor, sink = mixed[0:count // 2 * 2:2], mixed[1:count // 2 * 2:2]
    room = jnp.minimum(lengths[donor] - 1, reach - lengths[sink]) // 2
    room = jnp.where((donor == sequence[0]) | (sink == sequence[0]) | (lengths[sink] == 0), 0, jnp.maximum(room, 0))
    moved = jax.random.randint(jax.random.fold_in(own, 4), (count // 2,), 0, 1 << 20) % (room + 1)
    lengths = lengths.at[donor].add(-moved).at[sink].add(moved)
    items = jnp.searchsorted(jnp.cumsum(lengths), jnp.arange(rows * top), side="right").astype(jnp.int32)
    table = items.reshape(top, rows).T
    table = table[jax.random.permutation(jax.random.fold_in(own, 1), rows)]
    turn = jax.random.randint(jax.random.fold_in(own, 2), (rows, 1), 0, top)
    return jnp.take_along_axis(table, (jnp.arange(top)[None, :] + turn) % top, axis=1)


def load_shares(number_of, total, bound, lean, full):
    portions = [(1 << 20) // math.isqrt(rank ** lean) + 1 for rank in range(1, number_of + 1)]
    largest = bound if full else min(bound, max(-(-total // number_of), total * portions[0] // sum(portions)))
    least = 1 if total - largest >= number_of - 1 else 0
    given, surplus = [largest] + [least] * (number_of - 1), total - largest - least * (number_of - 1)
    while surplus > 0:
        movable = [i for i in range(1, number_of) if given[i] < largest] or [i for i in range(1, number_of) if given[i] < bound]
        mass, remaining = sum([portions[i] for i in movable]), surplus
        for i in movable:
            addition = min(bound - given[i], max(1, remaining * portions[i] // mass), surplus)
            given[i] = given[i] + addition
            surplus = surplus - addition
    return np.array(given)


def gaussian(rng, dims, deviation, most, cuts=(), kind=jnp.bfloat16):
    values = deviation * jax.random.normal(rng, dims, jnp.float32)
    if cuts:
        values = values * steps_of(rng, dims, cuts, -0.22, 0.18)
    return jnp.clip(values, -most, most).astype(kind)


def setup_inputs(seed: int = 0) -> dict:
    keys = jax.random.split(jax.random.key(seed), 8)
    inputs = gaussian(keys[0], (N_SECTION, TOKENS, D), 1.0, 6.0, ((0, 8), (1, 16)))
    out_grad = gaussian(keys[1], (N_SECTION, TOKENS, D), 1.0, 6.0, ((0, 8), (1, 16)))
    expert_ids_keys = jax.random.split(jax.random.fold_in(keys[2], 1), N_SECTION * TOKENS // TOK_DEV)
    expert_ids_turns = jax.random.permutation(jax.random.fold_in(keys[2], 3), N_SECTION * TOKENS // TOK_DEV)
    expert_ids = jax.vmap(lambda own, number: deal_out(jax.random.fold_in(keys[2], 2), own, number, TOK_DEV, EXPERTS, TOPK, CAP, 2))(expert_ids_keys, expert_ids_turns).reshape((N_SECTION, TOKENS, TOPK))
    gate_probs = jnp.clip(jnp.exp(math.log(0.59765625) - 2.4849066 * jax.random.uniform(keys[3], (N_SECTION, TOKENS, TOPK), jnp.float32) ** steps_of(keys[3], (N_SECTION, TOKENS, TOPK), ((0, 8), (1, 16)), -0.2, 0.2)), 0.049804688, 0.59765625).astype(jnp.bfloat16)
    gate_weight = gaussian(keys[4], (N_SECTION, EXPERTS, D, FF), D ** -0.5, 0.125, ((0, 8), (1, 16)))
    up_weight = gaussian(keys[5], (N_SECTION, EXPERTS, D, FF), D ** -0.5, 0.125, ((0, 8), (1, 16)))
    down_weight = gaussian(keys[6], (N_SECTION, EXPERTS, FF, D), FF ** -0.5, 0.21875, ((0, 8), (1, 16)))
    return dict(inputs=inputs, out_grad=out_grad, expert_ids=expert_ids, gate_probs=gate_probs, gate_weight=gate_weight, up_weight=up_weight, down_weight=down_weight)


def route_tables(expert_ids, experts, capacity):
    columns = jnp.arange(experts, dtype=jnp.int32)
    matches = expert_ids[:, :, None] == columns[None, None, :]
    member = jnp.sum(matches.astype(jnp.int32), axis=1)
    slot_rank = jnp.cumsum(member, axis=0) - member
    slot_index = jnp.arange(capacity, dtype=jnp.int32)
    placed = (member[:, :, None] == 1) & (slot_rank[:, :, None] == slot_index[None, None, :])
    return matches, placed


def expert_backward(rows_in, rows_grad, rows_gate, gate_mat, up_mat, down_mat):
    pre_gate = jnp.dot(rows_in, gate_mat, preferred_element_type=jnp.float32)
    pre_up = jnp.dot(rows_in, up_mat, preferred_element_type=jnp.float32)
    sig_gate = jax.nn.sigmoid(pre_gate)
    active = pre_gate * sig_gate
    hidden = active * pre_up
    down_back = jnp.dot(rows_grad, down_mat.T, preferred_element_type=jnp.float32)
    slot_grad = jnp.sum(hidden * down_back, axis=1).astype(jnp.bfloat16)
    weight = rows_gate.astype(jnp.float32)[:, None]
    scaled = weight * down_back
    hidden_gated = (weight * hidden).astype(jnp.bfloat16)
    down_wgrad = jnp.dot(hidden_gated.T, rows_grad, preferred_element_type=jnp.float32)
    grad_gate = (scaled * pre_up * sig_gate * (1.0 + pre_gate * (1.0 - sig_gate))).astype(jnp.bfloat16)
    grad_up = (scaled * active).astype(jnp.bfloat16)
    rows_back = (jnp.dot(grad_gate, gate_mat.T, preferred_element_type=jnp.float32)
                 + jnp.dot(grad_up, up_mat.T, preferred_element_type=jnp.float32)).astype(jnp.bfloat16)
    gate_wgrad = jnp.dot(rows_in.T, grad_gate, preferred_element_type=jnp.float32)
    up_wgrad = jnp.dot(rows_in.T, grad_up, preferred_element_type=jnp.float32)
    return (rows_back, slot_grad, gate_wgrad.astype(jnp.bfloat16),
            up_wgrad.astype(jnp.bfloat16), down_wgrad.astype(jnp.bfloat16))


def section_backward(section_args):
    inputs, out_grad, expert_ids, gate_probs, gate_weight, up_weight, down_weight = section_args
    id_blocks = expert_ids.reshape(N_EXPERT, TOK_DEV, TOPK)
    matches, placed = jax.vmap(lambda block: route_tables(block, EXPERTS, CAP))(id_blocks)
    gate_values = gate_probs.reshape(N_EXPERT, TOK_DEV, TOPK, 1).astype(jnp.float32)
    gate_table = jnp.sum(jnp.where(matches, gate_values, 0.0), axis=2)
    placed_wide = placed.astype(jnp.float32)
    inputs_wide = inputs.reshape(N_EXPERT, TOK_DEV, D).astype(jnp.float32)
    grads_wide = out_grad.reshape(N_EXPERT, TOK_DEV, D).astype(jnp.float32)

    def per_expert(expert):
        chosen = lax.dynamic_index_in_dim(placed_wide, expert, 2, keepdims=False)
        rows_in = jnp.einsum('jtc,jtd->jcd', chosen, inputs_wide).astype(jnp.bfloat16).reshape(N_EXPERT * CAP, D)
        rows_grad = jnp.einsum('jtc,jtd->jcd', chosen, grads_wide).astype(jnp.bfloat16).reshape(N_EXPERT * CAP, D)
        gate_column = lax.dynamic_index_in_dim(gate_table, expert, 2, keepdims=False)
        rows_gate = jnp.einsum('jtc,jt->jc', chosen, gate_column).astype(jnp.bfloat16).reshape(N_EXPERT * CAP)
        return expert_backward(rows_in, rows_grad, rows_gate, gate_weight[expert], up_weight[expert], down_weight[expert])

    rows_back, slot_grad, gate_wgrad, up_wgrad, down_wgrad = lax.map(per_expert, jnp.arange(EXPERTS, dtype=jnp.int32))
    back_wide = lax.optimization_barrier(rows_back).astype(jnp.float32).reshape(EXPERTS, N_EXPERT, CAP, D)
    moe_sum = jnp.einsum('jtec,ejcd->jtd', placed_wide, back_wide)
    slot_wide = lax.optimization_barrier(slot_grad).astype(jnp.float32).reshape(EXPERTS, N_EXPERT, CAP)
    token_table = jnp.einsum('jtec,ejc->jte', placed_wide, slot_wide)
    gate_grad = jnp.sum(jnp.where(matches, token_table[:, :, None, :], 0.0), axis=3)
    gate_grad = gate_grad.astype(jnp.bfloat16).reshape(TOKENS, TOPK)
    moe_part = lax.optimization_barrier(moe_sum.astype(jnp.bfloat16)).astype(jnp.float32).reshape(TOKENS, D)
    section_grad = (out_grad.astype(jnp.float32) + moe_part).astype(jnp.bfloat16)
    return section_grad, gate_grad, gate_wgrad, up_wgrad, down_wgrad


def reference(inputs, out_grad, expert_ids, gate_probs, gate_weight, up_weight, down_weight):
    section_grad, gate_grad, gate_wgrad, up_wgrad, down_wgrad = lax.map(
        section_backward, (inputs, out_grad, expert_ids, gate_probs, gate_weight, up_weight, down_weight))
    handed_grad = jnp.concatenate([section_grad[1:], jnp.zeros_like(section_grad[:1])], axis=0)
    return (handed_grad, gate_grad, gate_wgrad, up_wgrad, down_wgrad)
```

```python
import functools

import jax
import jax.numpy as jnp
from jax import lax
from jax.experimental import pallas as pl
from jax.experimental.pallas import tpu as pltpu
from jax.sharding import PartitionSpec as P

SIDE = 4
CAP = 72
GROUP = SIDE * CAP
META = 8
BF16 = jnp.bfloat16
F32 = jnp.float32
VMEM = pl.BlockSpec(memory_space=pltpu.VMEM)
SMEM = pl.BlockSpec(memory_space=pltpu.SMEM)
BY_COLS = (((1,), (1,)), ((), ()))
BY_ROWS = (((0,), (0,)), ((), ()))


def shift(block, down, over):
    route = []
    for row in range(SIDE):
        for col in range(SIDE):
            to = (row + down) % SIDE * SIDE + (col + over) % SIDE
            route.append((row * SIDE + col, to))
    return lax.ppermute(block, "expert", route)


def params(mib=56):
    return pltpu.CompilerParams(vmem_limit_bytes=mib * 1024 * 1024)


def cost(flops, nbytes):
    return pl.CostEstimate(flops=flops, bytes_accessed=nbytes, transcendentals=0)


def slots(id_blocks, experts):
    hits = []
    for ids, expert in zip(id_blocks, experts):
        hits.append(jnp.sum(jnp.where(ids == expert, 1.0, 0.0), axis=0, keepdims=True))
    hit = jnp.concatenate(hits, axis=0)
    pad = -len(hits) % 8
    if pad:
        hit = jnp.concatenate([hit, jnp.zeros((pad, hit.shape[1]), F32)], axis=0)
    tokens = hit.shape[1]
    earlier = lax.broadcasted_iota(jnp.int32, (tokens, tokens), 0) < lax.broadcasted_iota(
        jnp.int32, (tokens, tokens), 1
    )
    before = jnp.where(earlier, 1.0, 0.0).astype(BF16)
    rank = jnp.dot(hit.astype(BF16), before, preferred_element_type=F32)
    slot = jnp.where(hit > 0.5, rank, -1.0)
    return [slot[i : i + 1] for i in range(len(hits))]


def one_hot(slot, rows, first=0):
    row = lax.broadcasted_iota(jnp.int32, (rows, slot.shape[1]), 0)
    wanted = jnp.where(slot >= 0.0, slot + first, -1.0).astype(jnp.int32)
    return jnp.where(row == wanted, 1.0, 0.0)


def as_float(expert):
    return expert.astype(F32)


def pack_kernel(x_ref, g_ref, ids_ref, gates_ref, a_ref, b_ref):
    tokens, width = x_ref.shape
    meta = jnp.concatenate(
        [
            ids_ref[...].astype(F32),
            gates_ref[...].astype(F32),
            jnp.zeros((META, width - 2 * tokens), F32),
        ],
        axis=1,
    ).astype(BF16)
    a_ref[0:tokens] = x_ref[...]
    a_ref[tokens : tokens + META] = meta
    b_ref[0:tokens] = g_ref[...]
    b_ref[tokens : tokens + META] = meta


def pack(x, g, ids, gates):
    tokens, width = x.shape
    out = jax.ShapeDtypeStruct((tokens + META, width), BF16)
    return pl.pallas_call(
        pack_kernel,
        out_shape=(out, out),
        in_specs=[VMEM] * 4,
        out_specs=(VMEM, VMEM),
        compiler_params=params(16),
        cost_estimate=cost(0, 4 * tokens * width * 2),
    )(x, g, ids, gates)


def select_kernel(tokens, who_ref, *refs):
    a_refs, b_refs, (a_out, b_out) = refs[:4], refs[4:8], refs[8:]
    width = a_out.shape[1]
    ids = [r[tokens : tokens + META, 0:tokens].astype(F32) for r in (*a_refs, *b_refs)]
    experts = [as_float(who_ref[0])] * 4 + [as_float(who_ref[1])] * 4
    slot = slots(ids, experts)
    for refs_of, out, part in ((a_refs, a_out, slot[:4]), (b_refs, b_out, slot[4:])):
        picks = [one_hot(s, CAP).astype(BF16) for s in part]
        for left in range(0, width, 512):
            rows = [
                jnp.dot(p, r[0:tokens, left : left + 512], preferred_element_type=F32)
                for p, r in zip(picks, refs_of)
            ]
            out[0:GROUP, left : left + 512] = jnp.concatenate(rows, axis=0).astype(BF16)
    meta = [r[tokens : tokens + META, 0 : 2 * tokens].astype(F32) for r in a_refs]
    meta.append(jnp.zeros((META, width - 8 * tokens), F32))
    a_out[GROUP : GROUP + META] = jnp.concatenate(meta, axis=1).astype(BF16)


def select(who, a, b, tokens):
    width = a[0].shape[1]
    return pl.pallas_call(
        functools.partial(select_kernel, tokens),
        out_shape=(
            jax.ShapeDtypeStruct((GROUP + META, width), BF16),
            jax.ShapeDtypeStruct((GROUP, width), BF16),
        ),
        in_specs=[SMEM] + [VMEM] * 8,
        out_specs=(VMEM, VMEM),
        compiler_params=params(24),
        cost_estimate=cost(4 * GROUP * tokens * width, 7_000_000),
    )(who, *a, *b)


def sources(a_refs, tokens, expert):
    ids, gates = [], []
    for ref in a_refs:
        for near in range(SIDE):
            left = 2 * tokens * near
            block = ref[GROUP : GROUP + META, left : left + 2 * tokens].astype(F32)
            ids.append(block[:, 0:tokens])
            gates.append(block[:, tokens : 2 * tokens])
    slot = slots(ids, [expert] * len(ids))
    gate = [
        jnp.sum(jnp.where(i == expert, v, 0.0), axis=0, keepdims=True) for i, v in zip(ids, gates)
    ]
    return slot, gate


def expert_kernel(tokens, who_ref, *refs):
    a_refs, b_refs, (wg, wu, wd) = refs[:4], refs[4:8], refs[8:11]
    gg_out, gu_out, hg_out = refs[11:14]
    first_out, second_out = refs[14:18], refs[18:22]
    pg, pu, db, total, gate, slot_sum = refs[22:]
    step, last = pl.program_id(0), pl.num_programs(0) - 1
    half = first_out[0].shape[1]

    @pl.when(step == 0)
    def _():
        slot, value = sources(a_refs, tokens, as_float(who_ref[0]))
        for j in range(16):
            column = jnp.sum(one_hot(slot[j], CAP) * value[j], axis=1, keepdims=True)
            gate[j * CAP : (j + 1) * CAP] = column
        slot_sum[...] = jnp.zeros_like(slot_sum)

    for k in range(SIDE):
        at = slice(k * GROUP, (k + 1) * GROUP)
        rows = a_refs[k][0:GROUP]
        pg[at] = jnp.dot(rows, wg[...], preferred_element_type=F32)
        pu[at] = jnp.dot(rows, wu[...], preferred_element_type=F32)
        db[at] = lax.dot_general(b_refs[k][...], wd[...], BY_COLS, preferred_element_type=F32)

    def block(j, carry):
        here = pl.ds(pl.multiple_of(j * CAP, 8), CAP)
        there = pl.ds(pl.multiple_of((j % SIDE) * GROUP + (j // SIDE) * CAP, 8), CAP)
        pre_gate, pre_up, down_back = pg[here], pu[here], db[there]
        weight = gate[here]
        sig = jax.nn.sigmoid(pre_gate)
        active = pre_gate * sig
        hidden = active * pre_up
        slot_sum[here] += jnp.sum(hidden * down_back, axis=1, keepdims=True)
        scaled = weight * down_back
        pg[here] = scaled * pre_up * sig * (1.0 + pre_gate * (1.0 - sig))
        pu[here] = scaled * active
        db[there] = weight * hidden
        return carry

    lax.fori_loop(0, 16, block, 0)
    hg_out[...] = db[...].astype(BF16)
    for k in range(SIDE):
        at = slice(k * GROUP, (k + 1) * GROUP)
        grad_gate, grad_up = pg[at].astype(BF16), pu[at].astype(BF16)
        gg_out[at] = grad_gate
        gu_out[at] = grad_up
        for left in range(0, 2 * half, 512):
            cols = slice(left, left + 512)
            back = lax.dot_general(
                grad_gate, wg[cols], BY_COLS, preferred_element_type=F32
            ) + lax.dot_general(grad_up, wu[cols], BY_COLS, preferred_element_type=F32)

            @pl.when(step == 0)
            def _():
                total[at, cols] = back

            @pl.when(step > 0)
            def _():
                total[at, cols] += back

    @pl.when(step == last)
    def _():
        slot, _ = sources(a_refs, tokens, as_float(who_ref[0]))
        for k in range(SIDE):
            first_out[k][0:GROUP] = total[k * GROUP : (k + 1) * GROUP, 0:half].astype(BF16)
            lines = []
            for near in range(SIDE):
                j = k * SIDE + near
                value = slot_sum[j * CAP : (j + 1) * CAP].astype(BF16).astype(F32)
                lines.append(
                    jnp.sum(one_hot(slot[j], CAP) * value, axis=0, keepdims=True)
                )
            lines.append(jnp.zeros((META - SIDE, tokens), F32))
            table = jnp.concatenate(lines, axis=0)
            table = jnp.concatenate([table, jnp.zeros((META, half - tokens), F32)], axis=1)
            first_out[k][GROUP : GROUP + META] = table.astype(BF16)
            rows = [
                total[m * GROUP + k * CAP : m * GROUP + (k + 1) * CAP, half : 2 * half]
                for m in range(SIDE)
            ]
            second_out[k][...] = jnp.concatenate(rows, axis=0).astype(BF16)


def expert(who, a, b, wg, wu, wd, tokens):
    width, hidden = wg.shape
    tile = 256
    rows, half = SIDE * GROUP, width // 2
    whole = lambda n, m: pl.BlockSpec((n, m), lambda f: (0, 0), pipeline_mode=pl.Buffered(1))
    column = lambda n: pl.BlockSpec((n, tile), lambda f: (0, f))
    fixed = lambda n, m: pl.BlockSpec((n, m), lambda f: (0, 0))
    return pl.pallas_call(
        functools.partial(expert_kernel, tokens),
        grid=(hidden // tile,),
        out_shape=(
            [jax.ShapeDtypeStruct((rows, hidden), BF16)] * 3
            + [jax.ShapeDtypeStruct((GROUP + META, half), BF16)] * SIDE
            + [jax.ShapeDtypeStruct((GROUP, half), BF16)] * SIDE
        ),
        in_specs=(
            [SMEM]
            + [whole(GROUP + META, width)] * SIDE
            + [whole(GROUP, width)] * SIDE
            + [column(width), column(width), pl.BlockSpec((tile, width), lambda f: (f, 0))]
        ),
        out_specs=(
            [column(rows)] * 3
            + [fixed(GROUP + META, half)] * SIDE
            + [fixed(GROUP, half)] * SIDE
        ),
        scratch_shapes=[pltpu.VMEM((rows, tile), F32)] * 3
        + [pltpu.VMEM((rows, width), F32)]
        + [pltpu.VMEM((rows, 1), F32)] * 2,
        compiler_params=params(60),
        cost_estimate=cost(10 * rows * width * hidden, 32_000_000),
    )(who, *a, *b, wg, wu, wd)


def wgrad_kernel(*refs):
    a_refs, b_refs, (gg, gu, hg) = refs[:4], refs[4:8], refs[8:11]
    gate_out, up_out, down_out = refs[11:]
    a = jnp.concatenate([r[0:GROUP] for r in a_refs], axis=0)
    gate_out[...] = lax.dot_general(a, gg[...], BY_ROWS, preferred_element_type=F32).astype(BF16)
    up_out[...] = lax.dot_general(a, gu[...], BY_ROWS, preferred_element_type=F32).astype(BF16)
    b = jnp.concatenate([r[...] for r in b_refs], axis=0)
    down_out[...] = lax.dot_general(hg[...], b, BY_ROWS, preferred_element_type=F32).astype(BF16)


def wgrads(a, b, gg, gu, hg):
    rows, hidden = gg.shape
    width = a[0].shape[1]
    tile = 256
    whole = pl.BlockSpec((rows, hidden), lambda d: (0, 0), pipeline_mode=pl.Buffered(1))
    return pl.pallas_call(
        wgrad_kernel,
        grid=(width // tile,),
        out_shape=(
            jax.ShapeDtypeStruct((width, hidden), BF16),
            jax.ShapeDtypeStruct((width, hidden), BF16),
            jax.ShapeDtypeStruct((hidden, width), BF16),
        ),
        in_specs=[pl.BlockSpec((GROUP + META, tile), lambda d: (0, d))] * SIDE
        + [pl.BlockSpec((GROUP, tile), lambda d: (0, d))] * SIDE
        + [whole] * 3,
        out_specs=(
            pl.BlockSpec((tile, hidden), lambda d: (d, 0)),
            pl.BlockSpec((tile, hidden), lambda d: (d, 0)),
            pl.BlockSpec((hidden, tile), lambda d: (0, d)),
        ),
        compiler_params=params(40),
        cost_estimate=cost(6 * rows * width * hidden, 24_000_000),
    )(*a, *b, gg, gu, hg)


def gather_kernel(tokens, tables, who_ref, *refs):
    id_refs, back_refs, outs = refs[:4], refs[4:8], refs[8:]
    half = back_refs[0].shape[1]
    ids = [r[tokens : tokens + META, 0:tokens].astype(F32) for r in id_refs]
    pairs = [(near, far) for near in range(SIDE) for far in range(SIDE)]
    slot = slots([ids[n] for n, _ in pairs], [as_float(who_ref[f]) for _, f in pairs])
    for near in range(SIDE):
        places = []
        for far in range(SIDE):
            spread = one_hot(slot[near * SIDE + far], GROUP, near * CAP)
            places.append(spread.T.astype(BF16))
        for left in range(0, half, 512):
            cols = slice(left, left + 512)
            part = jnp.dot(places[0], back_refs[0][0:GROUP, cols], preferred_element_type=F32)
            for far in range(1, SIDE):
                part += jnp.dot(
                    places[far], back_refs[far][0:GROUP, cols], preferred_element_type=F32
                )
            outs[near][0:tokens, cols] = part.astype(BF16)
        if tables:
            lines = [
                r[GROUP : GROUP + META, 0:tokens].astype(F32)[near : near + 1] for r in back_refs
            ]
            lines.append(jnp.zeros((META - SIDE, tokens), F32))
            table = jnp.concatenate(lines, axis=0)
            table = jnp.concatenate([table, jnp.zeros((META, half - tokens), F32)], axis=1)
            outs[near][tokens : tokens + META] = table.astype(BF16)


def gather(who, blocks, back, tokens, tables):
    half = back[0].shape[1]
    rows = tokens + META if tables else tokens
    return pl.pallas_call(
        functools.partial(gather_kernel, tokens, tables),
        out_shape=[jax.ShapeDtypeStruct((rows, half), BF16)] * SIDE,
        in_specs=[SMEM] + [VMEM] * 8,
        out_specs=[VMEM] * SIDE,
        compiler_params=params(24),
        cost_estimate=cost(32 * tokens * GROUP * half, 6_000_000),
    )(who, *blocks, *back)


def finish_kernel(tokens, who_ref, g_ref, ids_ref, *refs):
    firsts, seconds, (out, gate_out) = refs[:4], refs[4:8], refs[8:]
    half = firsts[0].shape[1]
    for parts, left in ((firsts, 0), (seconds, half)):
        cols = slice(left, left + half)
        moe = parts[0][0:tokens].astype(F32)
        for part in parts[1:]:
            moe += part[0:tokens].astype(F32)
        moe = moe.astype(BF16).astype(F32)
        out[:, cols] = (g_ref[:, cols].astype(F32) + moe).astype(BF16)
    ids = ids_ref[...]
    grad = jnp.zeros(ids.shape, F32)
    for near in range(SIDE):
        table = firsts[near][tokens : tokens + META, 0:tokens].astype(F32)
        for far in range(SIDE):
            grad += jnp.where(ids == who_ref[near * SIDE + far], table[far : far + 1], 0.0)
    gate_out[...] = grad.astype(BF16)


def finish(who, g, ids, firsts, seconds):
    tokens, width = g.shape
    return pl.pallas_call(
        functools.partial(finish_kernel, tokens),
        out_shape=(
            jax.ShapeDtypeStruct((tokens, width), BF16),
            jax.ShapeDtypeStruct(ids.shape, BF16),
        ),
        in_specs=[SMEM] + [VMEM] * 10,
        out_specs=(VMEM, VMEM),
        compiler_params=params(16),
        cost_estimate=cost(0, 3_500_000),
    )(who, g, ids, *firsts, *seconds)


def local(inputs, out_grad, expert_ids, gate_probs, gate_weight, up_weight, down_weight):
    x, g = inputs[0], out_grad[0]
    tokens = x.shape[0]
    ids, gates = expert_ids[0].T, gate_probs[0].T
    me = lax.axis_index("expert").astype(jnp.int32)
    row, col = me // SIDE, me % SIDE
    near = jnp.arange(SIDE, dtype=jnp.int32)
    same_row = row * SIDE + (col + near) % SIDE
    same_col = (row + near) % SIDE * SIDE + col
    all_experts = ((row + near[:, None]) % SIDE * SIDE + (col + near[None, :]) % SIDE).reshape(-1)

    a0, b0 = pack(x, g, ids, gates)
    a, b = [a0, None, None, None], [b0, None, None, None]
    for d in (2, 1, 3):
        a[d] = shift(a0, d, 0)
        b[d] = shift(b0, 0, d)

    rows_in, rows_grad = [None] * SIDE, [None] * SIDE
    for d in (2, 1, 3, 0):
        send_a, send_b = select(jnp.stack([same_row[d], same_col[d]]), a, b, tokens)
        rows_in[d] = shift(send_a, 0, d) if d else send_a
        rows_grad[d] = shift(send_b, d, 0) if d else send_b

    made = expert(
        me[None], rows_in, rows_grad, gate_weight[0, 0], up_weight[0, 0], down_weight[0, 0], tokens
    )
    gg, gu, hg = made[:3]
    first, second = list(made[3:7]), list(made[7:11])
    for d in (2, 1, 3):
        first[d] = shift(first[d], 0, -d)
        second[d] = shift(second[d], -d, 0)
    gate_wgrad, up_wgrad, down_wgrad = wgrads(rows_in, rows_grad, gg, gu, hg)

    first = gather(same_row, a, first, tokens, True)
    second = gather(same_col, b, second, tokens, False)
    first, second = list(first), list(second)
    for d in (2, 1, 3):
        first[d] = shift(first[d], -d, 0)
        second[d] = shift(second[d], 0, -d)
    section_grad, gate_grad = finish(all_experts, g, ids, first, second)

    sections = lax.axis_size("section")
    handed = lax.ppermute(section_grad, "section", [(i + 1, i) for i in range(sections - 1)])
    return (
        handed[None],
        gate_grad.T[None],
        gate_wgrad[None, None],
        up_wgrad[None, None],
        down_wgrad[None, None],
    )


def solution(mesh):
    rows, mats = P("section", "expert", None), P("section", "expert", None, None)
    return jax.shard_map(
        local,
        mesh=mesh,
        in_specs=(rows, rows, rows, rows, mats, mats, mats),
        out_specs=(rows, rows, mats, mats, mats),
        check_vma=False,
    )
```

```python
import functools

import jax
import jax.numpy as jnp
from jax import lax
from jax.experimental import pallas as pl
from jax.experimental.pallas import tpu as pltpu
from jax.sharding import PartitionSpec as P

SIDE = 4
CAP = 72
GROUP = SIDE * CAP
META = 8
BF16 = jnp.bfloat16
F32 = jnp.float32
VMEM = pl.BlockSpec(memory_space=pltpu.VMEM)
SMEM = pl.BlockSpec(memory_space=pltpu.SMEM)
BY_COLS = (((1,), (1,)), ((), ()))
BY_ROWS = (((0,), (0,)), ((), ()))


def shift(block, down, over):
    route = []
    for row in range(SIDE):
        for col in range(SIDE):
            to = (row + down) % SIDE * SIDE + (col + over) % SIDE
            route.append((row * SIDE + col, to))
    return lax.ppermute(block, "expert", route)


def params(mib=56):
    return pltpu.CompilerParams(vmem_limit_bytes=mib * 1024 * 1024)


def cost(flops, nbytes):
    return pl.CostEstimate(flops=flops, bytes_accessed=nbytes, transcendentals=0)


def slots(id_blocks, experts):
    hits = []
    for ids, expert in zip(id_blocks, experts):
        hits.append(jnp.sum(jnp.where(ids == expert, 1.0, 0.0), axis=0, keepdims=True))
    hit = jnp.concatenate(hits, axis=0)
    pad = -len(hits) % 8
    if pad:
        hit = jnp.concatenate([hit, jnp.zeros((pad, hit.shape[1]), F32)], axis=0)
    tokens = hit.shape[1]
    earlier = lax.broadcasted_iota(jnp.int32, (tokens, tokens), 0) < lax.broadcasted_iota(
        jnp.int32, (tokens, tokens), 1
    )
    before = jnp.where(earlier, 1.0, 0.0).astype(BF16)
    rank = jnp.dot(hit.astype(BF16), before, preferred_element_type=F32)
    slot = jnp.where(hit > 0.5, rank, -1.0)
    return [slot[i : i + 1] for i in range(len(hits))]


def one_hot(slot, rows, first=0):
    row = lax.broadcasted_iota(jnp.int32, (rows, slot.shape[1]), 0)
    wanted = jnp.where(slot >= 0.0, slot + first, -1.0).astype(jnp.int32)
    return jnp.where(row == wanted, 1.0, 0.0)


def as_float(expert):
    return expert.astype(F32)


def after(value, *others):
    return lax.optimization_barrier((value, *others))[0]


def ahead(me, down, over):
    row = lax.rem(lax.shift_right_logical(me, 2) + down, SIDE)
    col = lax.rem(lax.bitwise_and(me, SIDE - 1) + over, SIDE)
    return row * SIDE + col


def pack_kernel(x_ref, g_ref, ids_ref, gates_ref, a_ref, b_ref, ids, gates, sems):
    tokens, width = a_ref.shape[0] - META, a_ref.shape[1]
    copies = [
        pltpu.make_async_copy(ids_ref, ids, sems.at[0]),
        pltpu.make_async_copy(gates_ref, gates, sems.at[1]),
        pltpu.make_async_copy(x_ref, a_ref.at[0:tokens], sems.at[2]),
        pltpu.make_async_copy(g_ref, b_ref.at[0:tokens], sems.at[3]),
    ]
    for copy in copies:
        copy.start()
    for copy in copies:
        copy.wait()
    meta = jnp.concatenate(
        [
            ids[...].astype(F32),
            gates[...].astype(F32),
            jnp.zeros((META, width - 2 * tokens), F32),
        ],
        axis=1,
    ).astype(BF16)
    a_ref[tokens : tokens + META] = meta
    b_ref[tokens : tokens + META] = meta


def pack(x, g, ids, gates):
    tokens, width = x.shape
    out = jax.ShapeDtypeStruct((tokens + META, width), BF16)
    return pl.pallas_call(
        pack_kernel,
        out_shape=(out, out),
        in_specs=[pl.BlockSpec(memory_space=pl.ANY)] * 4,
        out_specs=(VMEM, VMEM),
        scratch_shapes=[
            pltpu.VMEM(ids.shape, jnp.int32),
            pltpu.VMEM(gates.shape, BF16),
            pltpu.SemaphoreType.DMA((4,)),
        ],
        compiler_params=params(56),
        cost_estimate=cost(0, 4 * tokens * width * 2),
    )(x, g, ids, gates)


def select_kernel(tokens, step, who_ref, *refs):
    a_refs, b_refs, (a_out, b_out) = refs[:4], refs[4:8], refs[8:]
    width = a_out.shape[1]
    ids = [r[tokens : tokens + META, 0:tokens].astype(F32) for r in (*a_refs, *b_refs)]
    me = who_ref[0]
    experts = [as_float(ahead(me, 0, step))] * 4 + [as_float(ahead(me, step, 0))] * 4
    slot = slots(ids, experts)
    for refs_of, out, part in ((a_refs, a_out, slot[:4]), (b_refs, b_out, slot[4:])):
        picks = [one_hot(s, CAP).astype(BF16) for s in part]
        for left in range(0, width, 512):
            rows = [
                jnp.dot(p, r[0:tokens, left : left + 512], preferred_element_type=F32)
                for p, r in zip(picks, refs_of)
            ]
            out[0:GROUP, left : left + 512] = jnp.concatenate(rows, axis=0).astype(BF16)
    meta = [r[tokens : tokens + META, 0 : 2 * tokens].astype(F32) for r in a_refs]
    meta.append(jnp.zeros((META, width - 8 * tokens), F32))
    a_out[GROUP : GROUP + META] = jnp.concatenate(meta, axis=1).astype(BF16)


def select(who, step, a, b, tokens):
    width = a[0].shape[1]
    return pl.pallas_call(
        functools.partial(select_kernel, tokens, step),
        out_shape=(
            jax.ShapeDtypeStruct((GROUP + META, width), BF16),
            jax.ShapeDtypeStruct((GROUP, width), BF16),
        ),
        in_specs=[SMEM] + [VMEM] * 8,
        out_specs=(VMEM, VMEM),
        compiler_params=params(6),
        cost_estimate=cost(4 * GROUP * tokens * width, 7_000_000),
    )(who, *a, *b)


def ready_kernel(tokens, who_ref, a_ref, b_ref, wg, wu, wdt, pg, pu, db, gate, slot_out):
    me = as_float(who_ref[0])
    ids, value = [], []
    for near in range(SIDE):
        left = 2 * tokens * near
        block = a_ref[GROUP : GROUP + META, left : left + 2 * tokens].astype(F32)
        ids.append(block[:, 0:tokens])
        hit = block[:, 0:tokens] == me
        value.append(
            jnp.sum(jnp.where(hit, block[:, tokens : 2 * tokens], 0.0), axis=0, keepdims=True)
        )
    slot = slots(ids, [me] * SIDE)
    columns = [
        jnp.sum(one_hot(s, CAP) * v, axis=1, keepdims=True) for s, v in zip(slot, value)
    ]
    gate[...] = jnp.broadcast_to(jnp.concatenate(columns, axis=0), gate.shape)
    slot_out[...] = jnp.concatenate(slot + [jnp.zeros((8 - SIDE, tokens), F32)], axis=0)
    for left in range(0, pg.shape[1], 256):
        cols = slice(left, left + 256)
        rows = a_ref[0:GROUP]
        pg[:, cols] = jnp.dot(rows, wg[:, cols], preferred_element_type=F32)
        pu[:, cols] = jnp.dot(rows, wu[:, cols], preferred_element_type=F32)
        db[:, cols] = jnp.dot(b_ref[...], wdt[:, cols], preferred_element_type=F32)


def ready(who, a, b, wg, wu, wdt, tokens):
    width, hidden = wg.shape
    wide = jax.ShapeDtypeStruct((GROUP, hidden), F32)
    return pl.pallas_call(
        functools.partial(ready_kernel, tokens),
        out_shape=(
            wide,
            wide,
            wide,
            jax.ShapeDtypeStruct((GROUP, 128), F32),
            jax.ShapeDtypeStruct((8, tokens), F32),
        ),
        in_specs=[SMEM] + [VMEM] * 5,
        out_specs=[VMEM] * 5,
        compiler_params=params(8),
        cost_estimate=cost(6 * GROUP * width * hidden, 6_000_000),
    )(who, a, b, wg, wu, wdt)


def middle_kernel(tokens, *refs):
    pgs, pus, dbs, gates, slot_refs = (refs[4 * i : 4 * i + 4] for i in range(5))
    wgt, wut = refs[20:22]
    gg_out, gu_out, hg_out = refs[22:25]
    first_out, second_out = refs[25:29], refs[29:33]
    gg, gu, hg, back, slot_sum = refs[33:]
    half = first_out[0].shape[1]
    hidden_units = gg.shape[1]
    for k in range(SIDE):
        lines = []
        for near in range(SIDE):
            here = slice(near * CAP, (near + 1) * CAP)
            there = slice(k * CAP, (k + 1) * CAP)
            total = jnp.zeros((CAP, 1), F32)
            weight = gates[k][here, 0:1]
            for left in range(0, hidden_units, 256):
                cols = slice(left, left + 256)
                pre_gate, pre_up = pgs[k][here, cols], pus[k][here, cols]
                down_back = dbs[near][there, cols]
                sig = jax.nn.sigmoid(pre_gate)
                active = pre_gate * sig
                hidden = active * pre_up
                total += jnp.sum(hidden * down_back, axis=1, keepdims=True)
                scaled = weight * down_back
                gg[here, cols] = scaled * pre_up * sig * (1.0 + pre_gate * (1.0 - sig))
                gu[here, cols] = scaled * active
                row = near * GROUP + k * CAP
                hg[row : row + CAP, cols] = weight * hidden
            slot = slot_refs[k][near : near + 1]
            value = total.astype(BF16).astype(F32)
            lines.append(jnp.sum(one_hot(slot, CAP) * value, axis=0, keepdims=True))
        at = slice(k * GROUP, (k + 1) * GROUP)
        grad_gate, grad_up = gg[...].astype(BF16), gu[...].astype(BF16)
        gg_out[at] = grad_gate
        gu_out[at] = grad_up
        for left in range(0, 2 * half, 512):
            cols = slice(left, left + 512)
            rows = jnp.dot(grad_gate, wgt[:, cols], preferred_element_type=F32) + jnp.dot(
                grad_up, wut[:, cols], preferred_element_type=F32
            )
            if left < half:
                first_out[k][0:GROUP, cols] = rows.astype(BF16)
            else:
                back[at, left - half : left - half + 512] = rows
        lines.append(jnp.zeros((META - SIDE, tokens), F32))
        table = jnp.concatenate(lines, axis=0)
        table = jnp.concatenate([table, jnp.zeros((META, half - tokens), F32)], axis=1)
        first_out[k][GROUP : GROUP + META] = table.astype(BF16)
    for near in range(SIDE):
        rows = [back[k * GROUP + near * CAP : k * GROUP + (near + 1) * CAP] for k in range(SIDE)]
        second_out[near][...] = jnp.concatenate(rows, axis=0).astype(BF16)
    hg_out[...] = hg[...].astype(BF16)


def middle(pg, pu, db, gate, slot, wgt, wut, tokens):
    hidden, width = wgt.shape
    rows, half = SIDE * GROUP, width // 2
    return pl.pallas_call(
        functools.partial(middle_kernel, tokens),
        out_shape=(
            [jax.ShapeDtypeStruct((rows, hidden), BF16)] * 3
            + [jax.ShapeDtypeStruct((GROUP + META, half), BF16)] * SIDE
            + [jax.ShapeDtypeStruct((GROUP, half), BF16)] * SIDE
        ),
        in_specs=[VMEM] * 22,
        out_specs=[VMEM] * 11,
        scratch_shapes=[
            pltpu.VMEM((GROUP, hidden), F32),
            pltpu.VMEM((GROUP, hidden), F32),
            pltpu.VMEM((rows, hidden), F32),
            pltpu.VMEM((rows, half), F32),
            pltpu.VMEM((rows, 1), F32),
        ],
        compiler_params=params(14),
        cost_estimate=cost(4 * rows * width * hidden, 10_000_000),
    )(*pg, *pu, *db, *gate, *slot, wgt, wut)


def up_wgrad_kernel(*refs):
    a_refs, (gg, gu), (gate_out, up_out) = refs[:4], refs[4:6], refs[6:]
    a = jnp.concatenate([r[0:GROUP] for r in a_refs], axis=0)
    gate_out[...] = lax.dot_general(a, gg[...], BY_ROWS, preferred_element_type=F32).astype(BF16)
    up_out[...] = lax.dot_general(a, gu[...], BY_ROWS, preferred_element_type=F32).astype(BF16)


def up_wgrads(a, gg, gu):
    rows, hidden = gg.shape
    width = a[0].shape[1]
    tile = 256
    whole = pl.BlockSpec((rows, hidden), lambda d: (0, 0), pipeline_mode=pl.Buffered(1))
    return pl.pallas_call(
        up_wgrad_kernel,
        grid=(width // tile,),
        out_shape=[jax.ShapeDtypeStruct((width, hidden), BF16)] * 2,
        in_specs=[pl.BlockSpec((GROUP + META, tile), lambda d: (0, d))] * SIDE + [whole] * 2,
        out_specs=[pl.BlockSpec((tile, hidden), lambda d: (d, 0))] * 2,
        compiler_params=params(20),
        cost_estimate=cost(4 * rows * width * hidden, 15_000_000),
    )(*a, gg, gu)


def down_wgrad_kernel(*refs):
    b_refs, (hg, down_out) = refs[:4], refs[4:]
    b = jnp.concatenate([r[...] for r in b_refs], axis=0)
    down_out[...] = lax.dot_general(hg[...], b, BY_ROWS, preferred_element_type=F32).astype(BF16)


def down_wgrads(b, hg):
    rows, hidden = hg.shape
    width = b[0].shape[1]
    tile = 512
    return pl.pallas_call(
        down_wgrad_kernel,
        grid=(width // tile,),
        out_shape=jax.ShapeDtypeStruct((hidden, width), BF16),
        in_specs=[pl.BlockSpec((GROUP, tile), lambda d: (0, d))] * SIDE
        + [pl.BlockSpec((rows, hidden), lambda d: (0, 0), pipeline_mode=pl.Buffered(1))],
        out_specs=pl.BlockSpec((hidden, tile), lambda d: (0, d)),
        compiler_params=params(20),
        cost_estimate=cost(2 * rows * width * hidden, 10_000_000),
    )(*b, hg)


def gather_kernel(tokens, along_row, who_ref, *refs):
    id_refs, back_refs, outs = refs[:4], refs[4:8], refs[8:]
    half = back_refs[0].shape[1]
    ids = [r[tokens : tokens + META, 0:tokens].astype(F32) for r in id_refs]
    pairs = [(near, far) for near in range(SIDE) for far in range(SIDE)]
    me = who_ref[0]
    experts = [as_float(ahead(me, 0, f) if along_row else ahead(me, f, 0)) for f in range(SIDE)]
    slot = slots([ids[n] for n, _ in pairs], [experts[f] for _, f in pairs])
    for near in range(SIDE):
        places = []
        for far in range(SIDE):
            spread = one_hot(slot[near * SIDE + far], GROUP, near * CAP)
            places.append(spread.T.astype(BF16))
        for left in range(0, half, 512):
            cols = slice(left, left + 512)
            part = jnp.dot(places[0], back_refs[0][0:GROUP, cols], preferred_element_type=F32)
            for far in range(1, SIDE):
                part += jnp.dot(
                    places[far], back_refs[far][0:GROUP, cols], preferred_element_type=F32
                )
            outs[near][0:tokens, cols] = part.astype(BF16)
        if along_row:
            lines = [
                r[GROUP : GROUP + META, 0:tokens].astype(F32)[near : near + 1] for r in back_refs
            ]
            lines.append(jnp.zeros((META - SIDE, tokens), F32))
            table = jnp.concatenate(lines, axis=0)
            table = jnp.concatenate([table, jnp.zeros((META, half - tokens), F32)], axis=1)
            outs[near][tokens : tokens + META] = table.astype(BF16)


def gather(who, blocks, back, tokens, along_row):
    half = back[0].shape[1]
    rows = tokens + META if along_row else tokens
    return pl.pallas_call(
        functools.partial(gather_kernel, tokens, along_row),
        out_shape=[jax.ShapeDtypeStruct((rows, half), BF16)] * SIDE,
        in_specs=[SMEM] + [VMEM] * 8,
        out_specs=[VMEM] * SIDE,
        compiler_params=params(8),
        cost_estimate=cost(32 * tokens * GROUP * half, 6_000_000),
    )(who, *blocks, *back)


def finish_kernel(tokens, who_ref, g_ref, ids_ref, *refs):
    firsts, seconds, (out, gate_out) = refs[:4], refs[4:8], refs[8:]
    half = firsts[0].shape[1]
    for parts, left in ((firsts, 0), (seconds, half)):
        cols = slice(left, left + half)
        moe = parts[0][0:tokens].astype(F32)
        for part in parts[1:]:
            moe += part[0:tokens].astype(F32)
        moe = moe.astype(BF16).astype(F32)
        out[:, cols] = (g_ref[:, cols].astype(F32) + moe).astype(BF16)
    ids, me = ids_ref[...], who_ref[0]
    grad = jnp.zeros(ids.shape, F32)
    for near in range(SIDE):
        table = firsts[near][tokens : tokens + META, 0:tokens].astype(F32)
        for far in range(SIDE):
            grad += jnp.where(ids == ahead(me, near, far), table[far : far + 1], 0.0)
    gate_out[...] = grad.astype(BF16)


def finish(who, g, ids, firsts, seconds):
    tokens, width = g.shape
    return pl.pallas_call(
        functools.partial(finish_kernel, tokens),
        out_shape=(
            jax.ShapeDtypeStruct((tokens, width), BF16),
            jax.ShapeDtypeStruct(ids.shape, BF16),
        ),
        in_specs=[SMEM] + [VMEM] * 10,
        out_specs=(VMEM, VMEM),
        compiler_params=params(16),
        cost_estimate=cost(0, 3_500_000),
    )(who, g, ids, *firsts, *seconds)


def exchange(one, two, one_route, two_route, meanwhile=lambda: ()):
    one, two = list(one), list(two)
    for d in (1, 3, 2):
        one[d] = shift(one[d], *one_route(d))
    for d in (1, 3):
        two[d] = shift(two[d], *two_route(d))
    two[2] = shift(after(two[2], two[1], *meanwhile()), *two_route(2))
    return one, two


def local(inputs, out_grad, expert_ids, gate_probs, gate_weight, up_weight, down_weight):
    x, g = inputs[0], out_grad[0]
    tokens = x.shape[0]
    ids, gates = expert_ids[0].T, gate_probs[0].T
    who = lax.axis_index("expert").astype(jnp.int32)[None]

    a0, b0 = pack(x, g, ids, gates)
    wg, wu, wd = gate_weight[0, 0], up_weight[0, 0], down_weight[0, 0]
    wdt, wut = after(wd, a0).T, after(wu, a0).T
    a, b = exchange([a0] * SIDE, [b0] * SIDE, lambda d: (d, 0), lambda d: (0, d), lambda: (wdt,))
    wgt = after(wg, wut).T

    send_a, send_b, turn = [None] * SIDE, [None] * SIDE, after(who, wgt)
    for d in (1, 3, 2, 0):
        send_a[d], send_b[d] = select(turn, d, a, b, tokens)
        turn = after(who, send_a[d])
    own = ready(who, send_a[0], send_b[0], wg, wu, wdt, tokens)
    rows_in, rows_grad = exchange(
        send_a, send_b, lambda d: (0, d), lambda d: (d, 0), lambda: own[-1:]
    )

    made = [own]
    for d in (1, 2, 3):
        made.append(ready(who, rows_in[d], rows_grad[d], wg, wu, wdt, tokens))
    made = middle(*zip(*made), wgt, wut, tokens)
    gg, gu, hg = made[:3]
    down_wgrad = down_wgrads(rows_grad, hg)
    first, second = exchange(
        made[3:7], made[7:11], lambda d: (0, -d), lambda d: (-d, 0), lambda: (down_wgrad,)
    )
    gate_wgrad, up_wgrad = up_wgrads(rows_in, gg, gu)

    turn = after(who, gate_wgrad)
    first = gather(turn, a, first, tokens, True)
    second = gather(turn, b, second, tokens, False)
    first, second = exchange(first, second, lambda d: (-d, 0), lambda d: (0, -d))
    section_grad, gate_grad = finish(who, g, ids, first, second)

    sections = lax.axis_size("section")
    handed = lax.ppermute(section_grad, "section", [(i + 1, i) for i in range(sections - 1)])
    return (
        handed[None],
        gate_grad.T[None],
        gate_wgrad[None, None],
        up_wgrad[None, None],
        down_wgrad[None, None],
    )


def solution(mesh):
    rows, mats = P("section", "expert", None), P("section", "expert", None, None)
    return jax.shard_map(
        local,
        mesh=mesh,
        in_specs=(rows, rows, rows, rows, mats, mats, mats),
        out_specs=(rows, rows, mats, mats, mats),
        check_vma=False,
    )
```

```python
import functools

import jax
import jax.numpy as jnp
from jax import lax
from jax.experimental import pallas as pl
from jax.experimental.pallas import tpu as pltpu
from jax.sharding import PartitionSpec as P

SIDE = 4
CAP = 72
GROUP = SIDE * CAP
META = 8
BF16 = jnp.bfloat16
F32 = jnp.float32
VMEM = pl.BlockSpec(memory_space=pltpu.VMEM)
SMEM = pl.BlockSpec(memory_space=pltpu.SMEM)
BY_COLS = (((1,), (1,)), ((), ()))
BY_ROWS = (((0,), (0,)), ((), ()))


def shift(block, down, over):
    route = []
    for row in range(SIDE):
        for col in range(SIDE):
            to = (row + down) % SIDE * SIDE + (col + over) % SIDE
            route.append((row * SIDE + col, to))
    return lax.ppermute(block, "expert", route)


def params(mib=56):
    return pltpu.CompilerParams(vmem_limit_bytes=mib * 1024 * 1024)


def cost(flops, nbytes):
    return pl.CostEstimate(flops=flops, bytes_accessed=nbytes, transcendentals=0)


def slots(id_blocks, experts):
    hits = []
    for ids, expert in zip(id_blocks, experts):
        hits.append(jnp.sum(jnp.where(ids == expert, 1.0, 0.0), axis=0, keepdims=True))
    hit = jnp.concatenate(hits, axis=0)
    pad = -len(hits) % 8
    if pad:
        hit = jnp.concatenate([hit, jnp.zeros((pad, hit.shape[1]), F32)], axis=0)
    tokens = hit.shape[1]
    earlier = lax.broadcasted_iota(jnp.int32, (tokens, tokens), 0) < lax.broadcasted_iota(
        jnp.int32, (tokens, tokens), 1
    )
    before = jnp.where(earlier, 1.0, 0.0).astype(BF16)
    rank = jnp.dot(hit.astype(BF16), before, preferred_element_type=F32)
    slot = jnp.where(hit > 0.5, rank, -1.0)
    return [slot[i : i + 1] for i in range(len(hits))]


def one_hot(slot, rows, first=0):
    row = lax.broadcasted_iota(jnp.int32, (rows, slot.shape[1]), 0)
    wanted = jnp.where(slot >= 0.0, slot + first, -1.0).astype(jnp.int32)
    return jnp.where(row == wanted, 1.0, 0.0)


def as_float(expert):
    return expert.astype(F32)


def after(value, *others):
    return lax.optimization_barrier((value, *others))[0]


def ahead(me, down, over):
    row = lax.rem(lax.shift_right_logical(me, 2) + down, SIDE)
    col = lax.rem(lax.bitwise_and(me, SIDE - 1) + over, SIDE)
    return row * SIDE + col


def pack_kernel(x_ref, g_ref, ids_ref, gates_ref, a_ref, b_ref, ids, gates, sems):
    tokens, width = a_ref.shape[0] - META, a_ref.shape[1]
    copies = [
        pltpu.make_async_copy(ids_ref, ids, sems.at[0]),
        pltpu.make_async_copy(gates_ref, gates, sems.at[1]),
        pltpu.make_async_copy(x_ref, a_ref.at[0:tokens], sems.at[2]),
        pltpu.make_async_copy(g_ref, b_ref.at[0:tokens], sems.at[3]),
    ]
    for copy in copies:
        copy.start()
    for copy in copies:
        copy.wait()
    meta = jnp.concatenate(
        [
            ids[...].astype(F32),
            gates[...].astype(F32),
            jnp.zeros((META, width - 2 * tokens), F32),
        ],
        axis=1,
    ).astype(BF16)
    a_ref[tokens : tokens + META] = meta
    b_ref[tokens : tokens + META] = meta


def pack(x, g, ids, gates):
    tokens, width = x.shape
    out = jax.ShapeDtypeStruct((tokens + META, width), BF16)
    return pl.pallas_call(
        pack_kernel,
        out_shape=(out, out),
        in_specs=[pl.BlockSpec(memory_space=pl.ANY)] * 4,
        out_specs=(VMEM, VMEM),
        scratch_shapes=[
            pltpu.VMEM(ids.shape, jnp.int32),
            pltpu.VMEM(gates.shape, BF16),
            pltpu.SemaphoreType.DMA((4,)),
        ],
        compiler_params=params(56),
        cost_estimate=cost(0, 4 * tokens * width * 2),
    )(x, g, ids, gates)


def select_kernel(tokens, step, who_ref, *refs):
    a_refs, b_refs, (a_out, b_out) = refs[:4], refs[4:8], refs[8:]
    width = a_out.shape[1]
    ids = [r[tokens : tokens + META, 0:tokens].astype(F32) for r in (*a_refs, *b_refs)]
    me = who_ref[0]
    experts = [as_float(ahead(me, 0, step))] * 4 + [as_float(ahead(me, step, 0))] * 4
    slot = slots(ids, experts)
    for refs_of, out, part in ((a_refs, a_out, slot[:4]), (b_refs, b_out, slot[4:])):
        picks = [one_hot(s, CAP).astype(BF16) for s in part]
        for left in range(0, width, 512):
            rows = [
                jnp.dot(p, r[0:tokens, left : left + 512], preferred_element_type=F32)
                for p, r in zip(picks, refs_of)
            ]
            out[0:GROUP, left : left + 512] = jnp.concatenate(rows, axis=0).astype(BF16)
    meta = [r[tokens : tokens + META, 0 : 2 * tokens].astype(F32) for r in a_refs]
    meta.append(jnp.zeros((META, width - 8 * tokens), F32))
    a_out[GROUP : GROUP + META] = jnp.concatenate(meta, axis=1).astype(BF16)


def select(who, step, a, b, tokens):
    width = a[0].shape[1]
    return pl.pallas_call(
        functools.partial(select_kernel, tokens, step),
        out_shape=(
            jax.ShapeDtypeStruct((GROUP + META, width), BF16),
            jax.ShapeDtypeStruct((GROUP, width), BF16),
        ),
        in_specs=[SMEM] + [VMEM] * 8,
        out_specs=(VMEM, VMEM),
        compiler_params=params(24),
        cost_estimate=cost(4 * GROUP * tokens * width, 7_000_000),
    )(who, *a, *b)


def ready_kernel(tokens, who_ref, a_ref, b_ref, wg, wu, wdt, pg, pu, db, gate, slot_out):
    me = as_float(who_ref[0])
    ids, value = [], []
    for near in range(SIDE):
        left = 2 * tokens * near
        block = a_ref[GROUP : GROUP + META, left : left + 2 * tokens].astype(F32)
        ids.append(block[:, 0:tokens])
        hit = block[:, 0:tokens] == me
        value.append(
            jnp.sum(jnp.where(hit, block[:, tokens : 2 * tokens], 0.0), axis=0, keepdims=True)
        )
    slot = slots(ids, [me] * SIDE)
    columns = [
        jnp.sum(one_hot(s, CAP) * v, axis=1, keepdims=True) for s, v in zip(slot, value)
    ]
    gate[...] = jnp.broadcast_to(jnp.concatenate(columns, axis=0), gate.shape)
    slot_out[...] = jnp.concatenate(slot + [jnp.zeros((8 - SIDE, tokens), F32)], axis=0)
    for left in range(0, pg.shape[1], 256):
        cols = slice(left, left + 256)
        rows = a_ref[0:GROUP]
        pg[:, cols] = jnp.dot(rows, wg[:, cols], preferred_element_type=F32)
        pu[:, cols] = jnp.dot(rows, wu[:, cols], preferred_element_type=F32)
        db[:, cols] = jnp.dot(b_ref[...], wdt[:, cols], preferred_element_type=F32)


def ready(who, a, b, wg, wu, wdt, tokens):
    width, hidden = wg.shape
    wide = jax.ShapeDtypeStruct((GROUP, hidden), F32)
    return pl.pallas_call(
        functools.partial(ready_kernel, tokens),
        out_shape=(
            wide,
            wide,
            wide,
            jax.ShapeDtypeStruct((GROUP, 128), F32),
            jax.ShapeDtypeStruct((8, tokens), F32),
        ),
        in_specs=[SMEM] + [VMEM] * 5,
        out_specs=[VMEM] * 5,
        compiler_params=params(8),
        cost_estimate=cost(6 * GROUP * width * hidden, 6_000_000),
    )(who, a, b, wg, wu, wdt)


def middle_kernel(tokens, *refs):
    pgs, pus, dbs, gates, slot_refs = (refs[4 * i : 4 * i + 4] for i in range(5))
    wgt, wut = refs[20:22]
    gg_out, gu_out, hg_out = refs[22:25]
    first_out, second_out = refs[25:29], refs[29:33]
    gg, gu, hg, back, slot_sum = refs[33:]
    half = first_out[0].shape[1]
    hidden_units = gg.shape[1]
    for k in range(SIDE):
        lines = []
        for near in range(SIDE):
            here = slice(near * CAP, (near + 1) * CAP)
            there = slice(k * CAP, (k + 1) * CAP)
            total = jnp.zeros((CAP, 1), F32)
            weight = gates[k][here, 0:1]
            for left in range(0, hidden_units, 256):
                cols = slice(left, left + 256)
                pre_gate, pre_up = pgs[k][here, cols], pus[k][here, cols]
                down_back = dbs[near][there, cols]
                sig = jax.nn.sigmoid(pre_gate)
                active = pre_gate * sig
                hidden = active * pre_up
                total += jnp.sum(hidden * down_back, axis=1, keepdims=True)
                scaled = weight * down_back
                gg[here, cols] = scaled * pre_up * sig * (1.0 + pre_gate * (1.0 - sig))
                gu[here, cols] = scaled * active
                row = near * GROUP + k * CAP
                hg[row : row + CAP, cols] = weight * hidden
            slot = slot_refs[k][near : near + 1]
            value = total.astype(BF16).astype(F32)
            lines.append(jnp.sum(one_hot(slot, CAP) * value, axis=0, keepdims=True))
        at = slice(k * GROUP, (k + 1) * GROUP)
        grad_gate, grad_up = gg[...].astype(BF16), gu[...].astype(BF16)
        gg_out[at] = grad_gate
        gu_out[at] = grad_up
        for left in range(0, 2 * half, 512):
            cols = slice(left, left + 512)
            rows = jnp.dot(grad_gate, wgt[:, cols], preferred_element_type=F32) + jnp.dot(
                grad_up, wut[:, cols], preferred_element_type=F32
            )
            if left < half:
                first_out[k][0:GROUP, cols] = rows.astype(BF16)
            else:
                back[at, left - half : left - half + 512] = rows
        lines.append(jnp.zeros((META - SIDE, tokens), F32))
        table = jnp.concatenate(lines, axis=0)
        table = jnp.concatenate([table, jnp.zeros((META, half - tokens), F32)], axis=1)
        first_out[k][GROUP : GROUP + META] = table.astype(BF16)
    for near in range(SIDE):
        rows = [back[k * GROUP + near * CAP : k * GROUP + (near + 1) * CAP] for k in range(SIDE)]
        second_out[near][...] = jnp.concatenate(rows, axis=0).astype(BF16)
    hg_out[...] = hg[...].astype(BF16)


def middle(pg, pu, db, gate, slot, wgt, wut, tokens):
    hidden, width = wgt.shape
    rows, half = SIDE * GROUP, width // 2
    return pl.pallas_call(
        functools.partial(middle_kernel, tokens),
        out_shape=(
            [jax.ShapeDtypeStruct((rows, hidden), BF16)] * 3
            + [jax.ShapeDtypeStruct((GROUP + META, half), BF16)] * SIDE
            + [jax.ShapeDtypeStruct((GROUP, half), BF16)] * SIDE
        ),
        in_specs=[VMEM] * 22,
        out_specs=[VMEM] * 11,
        scratch_shapes=[
            pltpu.VMEM((GROUP, hidden), F32),
            pltpu.VMEM((GROUP, hidden), F32),
            pltpu.VMEM((rows, hidden), F32),
            pltpu.VMEM((rows, half), F32),
            pltpu.VMEM((rows, 1), F32),
        ],
        compiler_params=params(14),
        cost_estimate=cost(4 * rows * width * hidden, 10_000_000),
    )(*pg, *pu, *db, *gate, *slot, wgt, wut)


def up_wgrad_kernel(*refs):
    a_refs, (gg, gu), (gate_out, up_out) = refs[:4], refs[4:6], refs[6:]
    a = jnp.concatenate([r[0:GROUP] for r in a_refs], axis=0)
    gate_out[...] = lax.dot_general(a, gg[...], BY_ROWS, preferred_element_type=F32).astype(BF16)
    up_out[...] = lax.dot_general(a, gu[...], BY_ROWS, preferred_element_type=F32).astype(BF16)


def up_wgrads(a, gg, gu):
    rows, hidden = gg.shape
    width = a[0].shape[1]
    tile = 256
    whole = pl.BlockSpec((rows, hidden), lambda d: (0, 0), pipeline_mode=pl.Buffered(1))
    return pl.pallas_call(
        up_wgrad_kernel,
        grid=(width // tile,),
        out_shape=[jax.ShapeDtypeStruct((width, hidden), BF16)] * 2,
        in_specs=[pl.BlockSpec((GROUP + META, tile), lambda d: (0, d))] * SIDE + [whole] * 2,
        out_specs=[pl.BlockSpec((tile, hidden), lambda d: (d, 0))] * 2,
        compiler_params=params(20),
        cost_estimate=cost(4 * rows * width * hidden, 15_000_000),
    )(*a, gg, gu)


def down_wgrad_kernel(*refs):
    b_refs, (hg, down_out) = refs[:4], refs[4:]
    b = jnp.concatenate([r[...] for r in b_refs], axis=0)
    down_out[...] = lax.dot_general(hg[...], b, BY_ROWS, preferred_element_type=F32).astype(BF16)


def down_wgrads(b, hg):
    rows, hidden = hg.shape
    width = b[0].shape[1]
    tile = 512
    return pl.pallas_call(
        down_wgrad_kernel,
        grid=(width // tile,),
        out_shape=jax.ShapeDtypeStruct((hidden, width), BF16),
        in_specs=[pl.BlockSpec((GROUP, tile), lambda d: (0, d))] * SIDE
        + [pl.BlockSpec((rows, hidden), lambda d: (0, 0), pipeline_mode=pl.Buffered(1))],
        out_specs=pl.BlockSpec((hidden, tile), lambda d: (0, d)),
        compiler_params=params(20),
        cost_estimate=cost(2 * rows * width * hidden, 10_000_000),
    )(*b, hg)


def places_kernel(tokens, along_row, who_ref, *refs):
    id_refs, out = refs[:4], refs[4]
    ids = [r[tokens : tokens + META, 0:tokens].astype(F32) for r in id_refs]
    pairs = [(near, far) for near in range(SIDE) for far in range(SIDE)]
    me = who_ref[0]
    experts = [as_float(ahead(me, 0, f) if along_row else ahead(me, f, 0)) for f in range(SIDE)]
    slot = slots([ids[n] for n, _ in pairs], [experts[f] for _, f in pairs])
    for near in range(SIDE):
        spread = [one_hot(slot[near * SIDE + far], GROUP, near * CAP) for far in range(SIDE)]
        out[near * tokens : (near + 1) * tokens] = jnp.concatenate(spread, axis=0).T.astype(BF16)


def places(who, blocks, tokens, along_row):
    return pl.pallas_call(
        functools.partial(places_kernel, tokens, along_row),
        out_shape=jax.ShapeDtypeStruct((SIDE * tokens, SIDE * GROUP), BF16),
        in_specs=[SMEM] + [VMEM] * 4,
        out_specs=VMEM,
        compiler_params=params(6),
        cost_estimate=cost(0, 4_000_000),
    )(who, *blocks)


def gather_kernel(tokens, along_row, places_ref, *refs):
    back_refs, outs = refs[:4], refs[4:]
    half = back_refs[0].shape[1]
    for left in range(0, half, 512):
        cols = slice(left, left + 512)
        rows = jnp.concatenate([r[0:GROUP, cols] for r in back_refs], axis=0)
        for near in range(SIDE):
            mine = places_ref[near * tokens : (near + 1) * tokens]
            part = jnp.dot(mine, rows, preferred_element_type=F32)
            outs[near][0:tokens, cols] = part.astype(BF16)
    if along_row:
        tables = [r[GROUP : GROUP + META, 0:tokens].astype(F32) for r in back_refs]
        for near in range(SIDE):
            lines = [t[near : near + 1] for t in tables]
            lines.append(jnp.zeros((META - SIDE, tokens), F32))
            table = jnp.concatenate(lines, axis=0)
            table = jnp.concatenate([table, jnp.zeros((META, half - tokens), F32)], axis=1)
            outs[near][tokens : tokens + META] = table.astype(BF16)


def gather(spots, back, tokens, along_row):
    half = back[0].shape[1]
    rows = tokens + META if along_row else tokens
    return pl.pallas_call(
        functools.partial(gather_kernel, tokens, along_row),
        out_shape=[jax.ShapeDtypeStruct((rows, half), BF16)] * SIDE,
        in_specs=[VMEM] * 5,
        out_specs=[VMEM] * SIDE,
        compiler_params=params(8),
        cost_estimate=cost(32 * tokens * GROUP * half, 6_000_000),
    )(spots, *back)


def finish_kernel(tokens, who_ref, g_ref, ids_ref, *refs):
    firsts, seconds, (out, gate_out) = refs[:4], refs[4:8], refs[8:]
    half = firsts[0].shape[1]
    for parts, left in ((firsts, 0), (seconds, half)):
        cols = slice(left, left + half)
        moe = parts[0][0:tokens].astype(F32)
        for part in parts[1:]:
            moe += part[0:tokens].astype(F32)
        moe = moe.astype(BF16).astype(F32)
        out[:, cols] = (g_ref[:, cols].astype(F32) + moe).astype(BF16)
    ids, me = ids_ref[...], who_ref[0]
    grad = jnp.zeros(ids.shape, F32)
    for near in range(SIDE):
        table = firsts[near][tokens : tokens + META, 0:tokens].astype(F32)
        for far in range(SIDE):
            grad += jnp.where(ids == ahead(me, near, far), table[far : far + 1], 0.0)
    gate_out[...] = grad.astype(BF16)


def finish(who, g, ids, firsts, seconds):
    tokens, width = g.shape
    return pl.pallas_call(
        functools.partial(finish_kernel, tokens),
        out_shape=(
            jax.ShapeDtypeStruct((tokens, width), BF16),
            jax.ShapeDtypeStruct(ids.shape, BF16),
        ),
        in_specs=[SMEM] + [VMEM] * 10,
        out_specs=(VMEM, VMEM),
        compiler_params=params(16),
        cost_estimate=cost(0, 3_500_000),
    )(who, g, ids, *firsts, *seconds)


def exchange(one, two, one_route, two_route, rounds, meanwhile=lambda: ()):
    one, two = list(one), list(two)
    for d in (1, 3):
        one[d] = shift(one[d], *one_route(d))
        two[d] = shift(two[d], *two_route(d))
    done = meanwhile()
    if rounds:
        one[2], two[2] = after(one[2], one[1], one[3], *done), after(two[2], two[1], two[3], *done)
    else:
        two[2] = after(two[2], two[1], *done)
    one[2], two[2] = shift(one[2], *one_route(2)), shift(two[2], *two_route(2))
    return one, two


def local(inputs, out_grad, expert_ids, gate_probs, gate_weight, up_weight, down_weight):
    x, g = inputs[0], out_grad[0]
    tokens = x.shape[0]
    ids, gates = expert_ids[0].T, gate_probs[0].T
    who = lax.axis_index("expert").astype(jnp.int32)[None]

    a0, b0 = pack(x, g, ids, gates)
    wg, wu, wd = gate_weight[0, 0], up_weight[0, 0], down_weight[0, 0]
    wdt, wut = after(wd, a0).T, after(wu, a0).T
    a, b = exchange([a0] * SIDE, [b0] * SIDE, lambda d: (d, 0), lambda d: (0, d), False, lambda: (wdt,))
    wgt = after(wg, wut).T

    send_a, send_b, turn = [None] * SIDE, [None] * SIDE, after(who, wgt)
    for d in (1, 3, 2, 0):
        send_a[d], send_b[d] = select(turn, d, a, b, tokens)
        turn = after(who, send_a[d])
    own = ready(who, send_a[0], send_b[0], wg, wu, wdt, tokens)
    rows_in, rows_grad = exchange(
        send_a, send_b, lambda d: (0, d), lambda d: (d, 0), True, lambda: own[-1:]
    )
    row_spots = places(after(who, own[-1]), a, tokens, True)
    col_spots = places(after(who, row_spots), b, tokens, False)

    made = [own]
    for d in (1, 2, 3):
        made.append(ready(who, rows_in[d], rows_grad[d], wg, wu, wdt, tokens))
    made = middle(*zip(*made), wgt, wut, tokens)
    gg, gu, hg = made[:3]
    down_wgrad = down_wgrads(rows_grad, hg)
    first, second = exchange(
        made[3:7], made[7:11], lambda d: (0, -d), lambda d: (-d, 0), False, lambda: (down_wgrad,)
    )
    gate_wgrad, up_wgrad = up_wgrads(rows_in, gg, gu)

    first = gather(after(row_spots, gate_wgrad), first, tokens, True)
    second = gather(after(col_spots, gate_wgrad), second, tokens, False)
    first, second = exchange(first, second, lambda d: (-d, 0), lambda d: (0, -d), False)
    section_grad, gate_grad = finish(who, g, ids, first, second)

    sections = lax.axis_size("section")
    handed = lax.ppermute(section_grad, "section", [(i + 1, i) for i in range(sections - 1)])
    return (
        handed[None],
        gate_grad.T[None],
        gate_wgrad[None, None],
        up_wgrad[None, None],
        down_wgrad[None, None],
    )


def solution(mesh):
    rows, mats = P("section", "expert", None), P("section", "expert", None, None)
    return jax.shard_map(
        local,
        mesh=mesh,
        in_specs=(rows, rows, rows, rows, mats, mats, mats),
        out_specs=(rows, rows, mats, mats, mats),
        check_vma=False,
    )
```

```python
import functools

import jax
import jax.numpy as jnp
from jax import lax
from jax.experimental import pallas as pl
from jax.experimental.pallas import tpu as pltpu
from jax.sharding import PartitionSpec as P

SIDE = 4
CAP = 72
GROUP = SIDE * CAP
META = 8
BF16 = jnp.bfloat16
F32 = jnp.float32
VMEM = pl.BlockSpec(memory_space=pltpu.VMEM)
SMEM = pl.BlockSpec(memory_space=pltpu.SMEM)
BY_COLS = (((1,), (1,)), ((), ()))
BY_ROWS = (((0,), (0,)), ((), ()))


def shift(block, down, over):
    route = []
    for row in range(SIDE):
        for col in range(SIDE):
            to = (row + down) % SIDE * SIDE + (col + over) % SIDE
            route.append((row * SIDE + col, to))
    return lax.ppermute(block, "expert", route)


def params(mib=56):
    return pltpu.CompilerParams(vmem_limit_bytes=mib * 1024 * 1024)


def cost(flops, nbytes):
    return pl.CostEstimate(flops=flops, bytes_accessed=nbytes, transcendentals=0)


def slots(id_blocks, experts):
    hits = []
    for ids, expert in zip(id_blocks, experts):
        hits.append(jnp.sum(jnp.where(ids == expert, 1.0, 0.0), axis=0, keepdims=True))
    hit = jnp.concatenate(hits, axis=0)
    pad = -len(hits) % 8
    if pad:
        hit = jnp.concatenate([hit, jnp.zeros((pad, hit.shape[1]), F32)], axis=0)
    tokens = hit.shape[1]
    earlier = lax.broadcasted_iota(jnp.int32, (tokens, tokens), 0) < lax.broadcasted_iota(
        jnp.int32, (tokens, tokens), 1
    )
    before = jnp.where(earlier, 1.0, 0.0).astype(BF16)
    rank = jnp.dot(hit.astype(BF16), before, preferred_element_type=F32)
    slot = jnp.where(hit > 0.5, rank, -1.0)
    return [slot[i : i + 1] for i in range(len(hits))]


def one_hot(slot, rows, first=0):
    row = lax.broadcasted_iota(jnp.int32, (rows, slot.shape[1]), 0)
    wanted = jnp.where(slot >= 0.0, slot + first, -1.0).astype(jnp.int32)
    return jnp.where(row == wanted, 1.0, 0.0)


def as_float(expert):
    return expert.astype(F32)


def after(value, *others):
    return lax.optimization_barrier((value, *others))[0]


def ahead(me, down, over):
    row = lax.rem(lax.shift_right_logical(me, 2) + down, SIDE)
    col = lax.rem(lax.bitwise_and(me, SIDE - 1) + over, SIDE)
    return row * SIDE + col


def pack_kernel(x_ref, g_ref, ids_ref, gates_ref, a_ref, b_ref, ids, gates, sems):
    tokens, width = a_ref.shape[0] - META, a_ref.shape[1]
    copies = [
        pltpu.make_async_copy(ids_ref, ids, sems.at[0]),
        pltpu.make_async_copy(gates_ref, gates, sems.at[1]),
        pltpu.make_async_copy(x_ref, a_ref.at[0:tokens], sems.at[2]),
        pltpu.make_async_copy(g_ref, b_ref.at[0:tokens], sems.at[3]),
    ]
    for copy in copies:
        copy.start()
    for copy in copies:
        copy.wait()
    meta = jnp.concatenate(
        [
            ids[...].astype(F32),
            gates[...].astype(F32),
            jnp.zeros((META, width - 2 * tokens), F32),
        ],
        axis=1,
    ).astype(BF16)
    a_ref[tokens : tokens + META] = meta
    b_ref[tokens : tokens + META] = meta


def pack(x, g, ids, gates):
    tokens, width = x.shape
    out = jax.ShapeDtypeStruct((tokens + META, width), BF16)
    return pl.pallas_call(
        pack_kernel,
        out_shape=(out, out),
        in_specs=[pl.BlockSpec(memory_space=pl.ANY)] * 4,
        out_specs=(VMEM, VMEM),
        scratch_shapes=[
            pltpu.VMEM(ids.shape, jnp.int32),
            pltpu.VMEM(gates.shape, BF16),
            pltpu.SemaphoreType.DMA((4,)),
        ],
        compiler_params=params(56),
        cost_estimate=cost(0, 4 * tokens * width * 2),
    )(x, g, ids, gates)


def pieces_kernel(*refs):
    sources, outs = refs[:4], refs[4:]
    for source, out in zip(sources[:2], outs[:2]):
        out[...] = source[0 : out.shape[0]]
    for source, out in zip(sources[2:], outs[2:]):
        rows = source.shape[0]
        out[...] = source[rows - out.shape[0] : rows]


def pieces(lows, highs, half):
    rows, width = lows[0].shape
    return pl.pallas_call(
        pieces_kernel,
        out_shape=[jax.ShapeDtypeStruct((half, width), BF16)] * 2
        + [jax.ShapeDtypeStruct((rows - half, width), BF16)] * 2,
        in_specs=[VMEM] * 4,
        out_specs=[VMEM] * 4,
        compiler_params=params(4),
        cost_estimate=cost(0, 2_000_000),
    )(*lows, *highs)


def meta_of(ref, width):
    return ref[ref.shape[0] - META : ref.shape[0], 0:width].astype(F32)


def tokens_of(refs, tokens, cols):
    own, one, low, high, three = refs
    far = jnp.concatenate([low[:, cols], high[0 : tokens - low.shape[0], cols]], axis=0)
    return own[0:tokens, cols], one[0:tokens, cols], far, three[0:tokens, cols]


def with_meta(refs):
    own, one, _, high, three = refs
    return own, one, high, three


def select_kernel(tokens, step, who_ref, *refs):
    a_refs, b_refs, (a_out, b_out) = refs[:5], refs[5:10], refs[10:]
    width = a_out.shape[1]
    ids = [meta_of(r, tokens) for r in (*with_meta(a_refs), *with_meta(b_refs))]
    me = who_ref[0]
    experts = [as_float(ahead(me, 0, step))] * 4 + [as_float(ahead(me, step, 0))] * 4
    slot = slots(ids, experts)
    for refs_of, out, part in ((a_refs, a_out, slot[:4]), (b_refs, b_out, slot[4:])):
        picks = [one_hot(s, CAP).astype(BF16) for s in part]
        for left in range(0, width, 512):
            given = tokens_of(refs_of, tokens, slice(left, left + 512))
            rows = [jnp.dot(p, r, preferred_element_type=F32) for p, r in zip(picks, given)]
            out[0:GROUP, left : left + 512] = jnp.concatenate(rows, axis=0).astype(BF16)
    meta = [meta_of(r, 2 * tokens) for r in with_meta(a_refs)]
    meta.append(jnp.zeros((META, width - 8 * tokens), F32))
    a_out[GROUP : GROUP + META] = jnp.concatenate(meta, axis=1).astype(BF16)


def select(who, step, a, b, tokens):
    width = a[0].shape[1]
    return pl.pallas_call(
        functools.partial(select_kernel, tokens, step),
        out_shape=(
            jax.ShapeDtypeStruct((GROUP + META, width), BF16),
            jax.ShapeDtypeStruct((GROUP, width), BF16),
        ),
        in_specs=[SMEM] + [VMEM] * 10,
        out_specs=(VMEM, VMEM),
        compiler_params=params(24),
        cost_estimate=cost(4 * GROUP * tokens * width, 7_000_000),
    )(who, *a, *b)


def ready_kernel(tokens, who_ref, a_ref, b_ref, wg, wu, wdt, pg, pu, db, gate, slot_out):
    me = as_float(who_ref[0])
    ids, value = [], []
    for near in range(SIDE):
        left = 2 * tokens * near
        block = a_ref[GROUP : GROUP + META, left : left + 2 * tokens].astype(F32)
        ids.append(block[:, 0:tokens])
        hit = block[:, 0:tokens] == me
        value.append(
            jnp.sum(jnp.where(hit, block[:, tokens : 2 * tokens], 0.0), axis=0, keepdims=True)
        )
    slot = slots(ids, [me] * SIDE)
    columns = [
        jnp.sum(one_hot(s, CAP) * v, axis=1, keepdims=True) for s, v in zip(slot, value)
    ]
    gate[...] = jnp.broadcast_to(jnp.concatenate(columns, axis=0), gate.shape)
    slot_out[...] = jnp.concatenate(slot + [jnp.zeros((8 - SIDE, tokens), F32)], axis=0)
    for left in range(0, pg.shape[1], 256):
        cols = slice(left, left + 256)
        rows = a_ref[0:GROUP]
        pg[:, cols] = jnp.dot(rows, wg[:, cols], preferred_element_type=F32)
        pu[:, cols] = jnp.dot(rows, wu[:, cols], preferred_element_type=F32)
        db[:, cols] = jnp.dot(b_ref[...], wdt[:, cols], preferred_element_type=F32)


def ready(who, a, b, wg, wu, wdt, tokens):
    width, hidden = wg.shape
    wide = jax.ShapeDtypeStruct((GROUP, hidden), F32)
    return pl.pallas_call(
        functools.partial(ready_kernel, tokens),
        out_shape=(
            wide,
            wide,
            wide,
            jax.ShapeDtypeStruct((GROUP, 128), F32),
            jax.ShapeDtypeStruct((8, tokens), F32),
        ),
        in_specs=[SMEM] + [VMEM] * 5,
        out_specs=[VMEM] * 5,
        compiler_params=params(8),
        cost_estimate=cost(6 * GROUP * width * hidden, 6_000_000),
    )(who, a, b, wg, wu, wdt)


def middle_kernel(tokens, *refs):
    pgs, pus, dbs, gates, slot_refs = (refs[4 * i : 4 * i + 4] for i in range(5))
    wgt, wut = refs[20:22]
    gg_out, gu_out, hg_out = refs[22:25]
    first_out, second_out = refs[25:29], refs[29:33]
    gg, gu, hg, back, slot_sum = refs[33:]
    half = first_out[0].shape[1]
    hidden_units = gg.shape[1]
    for k in range(SIDE):
        lines = []
        for near in range(SIDE):
            here = slice(near * CAP, (near + 1) * CAP)
            there = slice(k * CAP, (k + 1) * CAP)
            total = jnp.zeros((CAP, 1), F32)
            weight = gates[k][here, 0:1]
            for left in range(0, hidden_units, 256):
                cols = slice(left, left + 256)
                pre_gate, pre_up = pgs[k][here, cols], pus[k][here, cols]
                down_back = dbs[near][there, cols]
                sig = jax.nn.sigmoid(pre_gate)
                active = pre_gate * sig
                hidden = active * pre_up
                total += jnp.sum(hidden * down_back, axis=1, keepdims=True)
                scaled = weight * down_back
                gg[here, cols] = scaled * pre_up * sig * (1.0 + pre_gate * (1.0 - sig))
                gu[here, cols] = scaled * active
                row = near * GROUP + k * CAP
                hg[row : row + CAP, cols] = weight * hidden
            slot = slot_refs[k][near : near + 1]
            value = total.astype(BF16).astype(F32)
            lines.append(jnp.sum(one_hot(slot, CAP) * value, axis=0, keepdims=True))
        at = slice(k * GROUP, (k + 1) * GROUP)
        grad_gate, grad_up = gg[...].astype(BF16), gu[...].astype(BF16)
        gg_out[at] = grad_gate
        gu_out[at] = grad_up
        for left in range(0, 2 * half, 512):
            cols = slice(left, left + 512)
            rows = jnp.dot(grad_gate, wgt[:, cols], preferred_element_type=F32) + jnp.dot(
                grad_up, wut[:, cols], preferred_element_type=F32
            )
            if left < half:
                first_out[k][0:GROUP, cols] = rows.astype(BF16)
            else:
                back[at, left - half : left - half + 512] = rows
        lines.append(jnp.zeros((META - SIDE, tokens), F32))
        table = jnp.concatenate(lines, axis=0)
        table = jnp.concatenate([table, jnp.zeros((META, half - tokens), F32)], axis=1)
        first_out[k][GROUP : GROUP + META] = table.astype(BF16)
    for near in range(SIDE):
        rows = [back[k * GROUP + near * CAP : k * GROUP + (near + 1) * CAP] for k in range(SIDE)]
        second_out[near][...] = jnp.concatenate(rows, axis=0).astype(BF16)
    hg_out[...] = hg[...].astype(BF16)


def middle(pg, pu, db, gate, slot, wgt, wut, tokens):
    hidden, width = wgt.shape
    rows, half = SIDE * GROUP, width // 2
    return pl.pallas_call(
        functools.partial(middle_kernel, tokens),
        out_shape=(
            [jax.ShapeDtypeStruct((rows, hidden), BF16)] * 3
            + [jax.ShapeDtypeStruct((GROUP + META, half), BF16)] * SIDE
            + [jax.ShapeDtypeStruct((GROUP, half), BF16)] * SIDE
        ),
        in_specs=[VMEM] * 22,
        out_specs=[VMEM] * 11,
        scratch_shapes=[
            pltpu.VMEM((GROUP, hidden), F32),
            pltpu.VMEM((GROUP, hidden), F32),
            pltpu.VMEM((rows, hidden), F32),
            pltpu.VMEM((rows, half), F32),
            pltpu.VMEM((rows, 1), F32),
        ],
        compiler_params=params(14),
        cost_estimate=cost(4 * rows * width * hidden, 10_000_000),
    )(*pg, *pu, *db, *gate, *slot, wgt, wut)


def up_wgrad_kernel(*refs):
    a_refs, (gg, gu), (gate_out, up_out) = refs[:4], refs[4:6], refs[6:]
    a = jnp.concatenate([r[0:GROUP] for r in a_refs], axis=0)
    gate_out[...] = lax.dot_general(a, gg[...], BY_ROWS, preferred_element_type=F32).astype(BF16)
    up_out[...] = lax.dot_general(a, gu[...], BY_ROWS, preferred_element_type=F32).astype(BF16)


def up_wgrads(a, gg, gu):
    rows, hidden = gg.shape
    width = a[0].shape[1]
    tile = 256
    whole = pl.BlockSpec((rows, hidden), lambda d: (0, 0), pipeline_mode=pl.Buffered(1))
    return pl.pallas_call(
        up_wgrad_kernel,
        grid=(width // tile,),
        out_shape=[jax.ShapeDtypeStruct((width, hidden), BF16)] * 2,
        in_specs=[pl.BlockSpec((GROUP + META, tile), lambda d: (0, d))] * SIDE + [whole] * 2,
        out_specs=[pl.BlockSpec((tile, hidden), lambda d: (d, 0))] * 2,
        compiler_params=params(20),
        cost_estimate=cost(4 * rows * width * hidden, 15_000_000),
    )(*a, gg, gu)


def down_wgrad_kernel(*refs):
    b_refs, (hg, down_out) = refs[:4], refs[4:]
    b = jnp.concatenate([r[...] for r in b_refs], axis=0)
    down_out[...] = lax.dot_general(hg[...], b, BY_ROWS, preferred_element_type=F32).astype(BF16)


def down_wgrads(b, hg):
    rows, hidden = hg.shape
    width = b[0].shape[1]
    tile = 512
    return pl.pallas_call(
        down_wgrad_kernel,
        grid=(width // tile,),
        out_shape=jax.ShapeDtypeStruct((hidden, width), BF16),
        in_specs=[pl.BlockSpec((GROUP, tile), lambda d: (0, d))] * SIDE
        + [pl.BlockSpec((rows, hidden), lambda d: (0, 0), pipeline_mode=pl.Buffered(1))],
        out_specs=pl.BlockSpec((hidden, tile), lambda d: (0, d)),
        compiler_params=params(20),
        cost_estimate=cost(2 * rows * width * hidden, 10_000_000),
    )(*b, hg)


def places_kernel(tokens, along_row, who_ref, *refs):
    id_refs, out = refs[:4], refs[4]
    ids = [meta_of(r, tokens) for r in id_refs]
    pairs = [(near, far) for near in range(SIDE) for far in range(SIDE)]
    me = who_ref[0]
    experts = [as_float(ahead(me, 0, f) if along_row else ahead(me, f, 0)) for f in range(SIDE)]
    slot = slots([ids[n] for n, _ in pairs], [experts[f] for _, f in pairs])
    for near in range(SIDE):
        spread = [one_hot(slot[near * SIDE + far], GROUP, near * CAP) for far in range(SIDE)]
        out[near * tokens : (near + 1) * tokens] = jnp.concatenate(spread, axis=0).T.astype(BF16)


def places(who, blocks, tokens, along_row):
    return pl.pallas_call(
        functools.partial(places_kernel, tokens, along_row),
        out_shape=jax.ShapeDtypeStruct((SIDE * tokens, SIDE * GROUP), BF16),
        in_specs=[SMEM] + [VMEM] * 4,
        out_specs=VMEM,
        compiler_params=params(6),
        cost_estimate=cost(0, 4_000_000),
    )(who, *with_meta(blocks))


def gather_kernel(tokens, along_row, places_ref, *refs):
    back_refs, outs = refs[:4], refs[4:]
    half = back_refs[0].shape[1]
    for left in range(0, half, 512):
        cols = slice(left, left + 512)
        rows = jnp.concatenate([r[0:GROUP, cols] for r in back_refs], axis=0)
        for near in range(SIDE):
            mine = places_ref[near * tokens : (near + 1) * tokens]
            part = jnp.dot(mine, rows, preferred_element_type=F32)
            outs[near][0:tokens, cols] = part.astype(BF16)
    if along_row:
        tables = [r[GROUP : GROUP + META, 0:tokens].astype(F32) for r in back_refs]
        for near in range(SIDE):
            lines = [t[near : near + 1] for t in tables]
            lines.append(jnp.zeros((META - SIDE, tokens), F32))
            table = jnp.concatenate(lines, axis=0)
            table = jnp.concatenate([table, jnp.zeros((META, half - tokens), F32)], axis=1)
            outs[near][tokens : tokens + META] = table.astype(BF16)


def gather(spots, back, tokens, along_row):
    half = back[0].shape[1]
    rows = tokens + META if along_row else tokens
    return pl.pallas_call(
        functools.partial(gather_kernel, tokens, along_row),
        out_shape=[jax.ShapeDtypeStruct((rows, half), BF16)] * SIDE,
        in_specs=[VMEM] * 5,
        out_specs=[VMEM] * SIDE,
        compiler_params=params(8),
        cost_estimate=cost(32 * tokens * GROUP * half, 6_000_000),
    )(spots, *back)


def summed(tokens, g, parts):
    moe = parts[0][0:tokens].astype(F32)
    for part in parts[1:]:
        moe += part[0:tokens].astype(F32)
    moe = moe.astype(BF16).astype(F32)
    return (g.astype(F32) + moe).astype(BF16)


def finish_first_kernel(tokens, who_ref, g_ref, ids_ref, *refs):
    parts, (out, gate_out) = refs[:4], refs[4:]
    out[...] = summed(tokens, g_ref[:, 0 : out.shape[1]], parts)
    ids, me = ids_ref[...], who_ref[0]
    grad = jnp.zeros(ids.shape, F32)
    for near in range(SIDE):
        table = parts[near][tokens : tokens + META, 0:tokens].astype(F32)
        for far in range(SIDE):
            grad += jnp.where(ids == ahead(me, near, far), table[far : far + 1], 0.0)
    gate_out[...] = grad.astype(BF16)


def finish_first(who, g, ids, parts):
    tokens = g.shape[0]
    return pl.pallas_call(
        functools.partial(finish_first_kernel, tokens),
        out_shape=(
            jax.ShapeDtypeStruct((tokens, parts[0].shape[1]), BF16),
            jax.ShapeDtypeStruct(ids.shape, BF16),
        ),
        in_specs=[SMEM] + [VMEM] * 6,
        out_specs=(VMEM, VMEM),
        compiler_params=params(4),
        cost_estimate=cost(0, 2_000_000),
    )(who, g, ids, *parts)


def finish_second_kernel(tokens, g_ref, *refs):
    parts, out = refs[:4], refs[4]
    half = out.shape[1]
    out[...] = summed(tokens, g_ref[:, half : 2 * half], parts)


def finish_second(g, parts):
    tokens = g.shape[0]
    return pl.pallas_call(
        functools.partial(finish_second_kernel, tokens),
        out_shape=jax.ShapeDtypeStruct((tokens, parts[0].shape[1]), BF16),
        in_specs=[VMEM] * 5,
        out_specs=VMEM,
        compiler_params=params(4),
        cost_estimate=cost(0, 2_000_000),
    )(g, *parts)


def exchange(one, two, one_route, two_route, rounds, meanwhile=lambda: ()):
    one, two = list(one), list(two)
    for d in (1, 3):
        one[d] = shift(one[d], *one_route(d))
        two[d] = shift(two[d], *two_route(d))
    done = meanwhile()
    if rounds:
        near = (one[1], one[3], two[1], two[3])
        one[2], two[2] = after(one[2], *near, *done), after(two[2], *near, *done)
    else:
        two[2] = after(two[2], two[1], *done)
    one[2], two[2] = shift(one[2], *one_route(2)), shift(two[2], *two_route(2))
    return one, two


def local(inputs, out_grad, expert_ids, gate_probs, gate_weight, up_weight, down_weight):
    x, g = inputs[0], out_grad[0]
    tokens = x.shape[0]
    ids, gates = expert_ids[0].T, gate_probs[0].T
    who = lax.axis_index("expert").astype(jnp.int32)[None]

    a0, b0 = pack(x, g, ids, gates)
    wg, wu, wd = gate_weight[0, 0], up_weight[0, 0], down_weight[0, 0]
    wdt, wut = after(wd, a0).T, after(wu, a0).T
    a1, b1, a3, b3 = shift(a0, 1, 0), shift(b0, 0, 1), shift(a0, 3, 0), shift(b0, 0, 3)
    half = tokens // 2
    a_low, b_low, a_high, b_high = pieces((after(a1, wdt), b1), (a3, b3), half)
    a_low, b_low = shift(a_low, 1, 0), shift(b_low, 0, 1)
    a_high, b_high = shift(a_high, 3, 0), shift(b_high, 0, 3)
    a, b = (a0, a1, a_low, a_high, a3), (b0, b1, b_low, b_high, b3)
    wgt = after(wg, wut).T

    send_a, send_b, turn = [None] * SIDE, [None] * SIDE, after(who, wgt)
    for d in (1, 3, 2, 0):
        send_a[d], send_b[d] = select(turn, d, a, b, tokens)
        turn = after(who, send_a[d])
    own = ready(who, send_a[0], send_b[0], wg, wu, wdt, tokens)
    row_spots = places(after(who, own[-1]), a, tokens, True)
    col_spots = places(after(who, row_spots), b, tokens, False)
    rows_in, rows_grad = exchange(
        send_a, send_b, lambda d: (0, d), lambda d: (d, 0), True, lambda: (own[-1], col_spots)
    )

    made = [own]
    for d in (1, 2, 3):
        made.append(ready(who, rows_in[d], rows_grad[d], wg, wu, wdt, tokens))
    made = middle(*zip(*made), wgt, wut, tokens)
    gg, gu, hg = made[:3]
    down_wgrad = down_wgrads(rows_grad, hg)
    first, second = exchange(
        made[3:7], made[7:11], lambda d: (0, -d), lambda d: (-d, 0), False, lambda: (down_wgrad,)
    )
    gate_wgrad, up_wgrad = up_wgrads(rows_in, gg, gu)

    first = gather(after(row_spots, gate_wgrad), first, tokens, True)
    second = gather(after(col_spots, gate_wgrad), second, tokens, False)
    first, second = exchange(first, second, lambda d: (-d, 0), lambda d: (0, -d), False)
    sections = lax.axis_size("section")
    back_one = [(i + 1, i) for i in range(sections - 1)]
    handed_second = lax.ppermute(finish_second(g, second), "section", back_one)
    grad_first, gate_grad = finish_first(who, g, ids, first)
    handed_first = lax.ppermute(grad_first, "section", back_one)
    handed = jnp.concatenate([handed_first, handed_second], axis=1)
    return (
        handed[None],
        gate_grad.T[None],
        gate_wgrad[None, None],
        up_wgrad[None, None],
        down_wgrad[None, None],
    )


def solution(mesh):
    rows, mats = P("section", "expert", None), P("section", "expert", None, None)
    return jax.shard_map(
        local,
        mesh=mesh,
        in_specs=(rows, rows, rows, rows, mats, mats, mats),
        out_specs=(rows, rows, mats, mats, mats),
        check_vma=False,
    )
```

```python
import functools

import jax
import jax.numpy as jnp
from jax import lax
from jax.experimental import pallas as pl
from jax.experimental.pallas import tpu as pltpu
from jax.sharding import PartitionSpec as P

SIDE = 4
CAP = 72
GROUP = SIDE * CAP
META = 8
BF16 = jnp.bfloat16
F32 = jnp.float32
VMEM = pl.BlockSpec(memory_space=pltpu.VMEM)
SMEM = pl.BlockSpec(memory_space=pltpu.SMEM)
BY_COLS = (((1,), (1,)), ((), ()))
BY_ROWS = (((0,), (0,)), ((), ()))


def shift(block, down, over):
    route = []
    for row in range(SIDE):
        for col in range(SIDE):
            to = (row + down) % SIDE * SIDE + (col + over) % SIDE
            route.append((row * SIDE + col, to))
    return lax.ppermute(block, "expert", route)


def params(mib=56):
    return pltpu.CompilerParams(vmem_limit_bytes=mib * 1024 * 1024)


def cost(flops, nbytes):
    return pl.CostEstimate(flops=flops, bytes_accessed=nbytes, transcendentals=0)


def slots(id_blocks, experts):
    hits = []
    for ids, expert in zip(id_blocks, experts):
        hits.append(jnp.sum(jnp.where(ids == expert, 1.0, 0.0), axis=0, keepdims=True))
    hit = jnp.concatenate(hits, axis=0)
    pad = -len(hits) % 8
    if pad:
        hit = jnp.concatenate([hit, jnp.zeros((pad, hit.shape[1]), F32)], axis=0)
    tokens = hit.shape[1]
    earlier = lax.broadcasted_iota(jnp.int32, (tokens, tokens), 0) < lax.broadcasted_iota(
        jnp.int32, (tokens, tokens), 1
    )
    before = jnp.where(earlier, 1.0, 0.0).astype(BF16)
    rank = jnp.dot(hit.astype(BF16), before, preferred_element_type=F32)
    slot = jnp.where(hit > 0.5, rank, -1.0)
    return [slot[i : i + 1] for i in range(len(hits))]


def one_hot(slot, rows, first=0):
    row = lax.broadcasted_iota(jnp.int32, (rows, slot.shape[1]), 0)
    wanted = jnp.where(slot >= 0.0, slot + first, -1.0).astype(jnp.int32)
    return jnp.where(row == wanted, 1.0, 0.0)


def as_float(expert):
    return expert.astype(F32)


def after(value, *others):
    return lax.optimization_barrier((value, *others))[0]


def ahead(me, down, over):
    row = lax.rem(lax.shift_right_logical(me, 2) + down, SIDE)
    col = lax.rem(lax.bitwise_and(me, SIDE - 1) + over, SIDE)
    return row * SIDE + col


def pack_kernel(x_ref, g_ref, ids_ref, gates_ref, a_ref, b_ref, ids, gates, sems):
    tokens, width = a_ref.shape[0] - META, a_ref.shape[1]
    copies = [
        pltpu.make_async_copy(ids_ref, ids, sems.at[0]),
        pltpu.make_async_copy(gates_ref, gates, sems.at[1]),
        pltpu.make_async_copy(x_ref, a_ref.at[0:tokens], sems.at[2]),
        pltpu.make_async_copy(g_ref, b_ref.at[0:tokens], sems.at[3]),
    ]
    for copy in copies:
        copy.start()
    for copy in copies:
        copy.wait()
    meta = jnp.concatenate(
        [
            ids[...].astype(F32),
            gates[...].astype(F32),
            jnp.zeros((META, width - 2 * tokens), F32),
        ],
        axis=1,
    ).astype(BF16)
    a_ref[tokens : tokens + META] = meta
    b_ref[tokens : tokens + META] = meta


def pack(x, g, ids, gates):
    tokens, width = x.shape
    out = jax.ShapeDtypeStruct((tokens + META, width), BF16)
    return pl.pallas_call(
        pack_kernel,
        out_shape=(out, out),
        in_specs=[pl.BlockSpec(memory_space=pl.ANY)] * 4,
        out_specs=(VMEM, VMEM),
        scratch_shapes=[
            pltpu.VMEM(ids.shape, jnp.int32),
            pltpu.VMEM(gates.shape, BF16),
            pltpu.SemaphoreType.DMA((4,)),
        ],
        compiler_params=params(56),
        cost_estimate=cost(0, 4 * tokens * width * 2),
    )(x, g, ids, gates)


def turn_kernel(in_ref, out_ref):
    out_ref[...] = in_ref[...].T


def turned(mat):
    rows, cols = mat.shape
    tile = 256
    tall = rows > cols
    down = pl.BlockSpec((tile, min(rows, cols)), lambda f: (f, 0))
    over = pl.BlockSpec((min(rows, cols), tile), lambda f: (0, f))
    return pl.pallas_call(
        turn_kernel,
        grid=(max(rows, cols) // tile,),
        out_shape=jax.ShapeDtypeStruct((cols, rows), BF16),
        in_specs=[down if tall else over],
        out_specs=over if tall else down,
        compiler_params=params(6),
        cost_estimate=cost(0, 4 * rows * cols),
    )(mat)


def pieces_kernel(*refs):
    sources, outs = refs[:4], refs[4:]
    for source, out in zip(sources[:2], outs[:2]):
        out[...] = source[0 : out.shape[0]]
    for source, out in zip(sources[2:], outs[2:]):
        rows = source.shape[0]
        out[...] = source[rows - out.shape[0] : rows]


def pieces(lows, highs, half):
    rows, width = lows[0].shape
    return pl.pallas_call(
        pieces_kernel,
        out_shape=[jax.ShapeDtypeStruct((half, width), BF16)] * 2
        + [jax.ShapeDtypeStruct((rows - half, width), BF16)] * 2,
        in_specs=[VMEM] * 4,
        out_specs=[VMEM] * 4,
        compiler_params=params(4),
        cost_estimate=cost(0, 2_000_000),
    )(*lows, *highs)


def meta_of(ref, width):
    return ref[ref.shape[0] - META : ref.shape[0], 0:width].astype(F32)


def tokens_of(refs, tokens, cols):
    own, one, low, high, three = refs
    far = jnp.concatenate([low[:, cols], high[0 : tokens - low.shape[0], cols]], axis=0)
    return own[0:tokens, cols], one[0:tokens, cols], far, three[0:tokens, cols]


def with_meta(refs):
    own, one, _, high, three = refs
    return own, one, high, three


def select_kernel(tokens, step, who_ref, *refs):
    a_refs, b_refs, (a_out, b_out) = refs[:5], refs[5:10], refs[10:]
    width = a_out.shape[1]
    ids = [meta_of(r, tokens) for r in (*with_meta(a_refs), *with_meta(b_refs))]
    me = who_ref[0]
    experts = [as_float(ahead(me, 0, step))] * 4 + [as_float(ahead(me, step, 0))] * 4
    slot = slots(ids, experts)
    for refs_of, out, part in ((a_refs, a_out, slot[:4]), (b_refs, b_out, slot[4:])):
        picks = [one_hot(s, CAP).astype(BF16) for s in part]
        for left in range(0, width, 512):
            given = tokens_of(refs_of, tokens, slice(left, left + 512))
            rows = [jnp.dot(p, r, preferred_element_type=F32) for p, r in zip(picks, given)]
            out[0:GROUP, left : left + 512] = jnp.concatenate(rows, axis=0).astype(BF16)
    meta = [meta_of(r, 2 * tokens) for r in with_meta(a_refs)]
    meta.append(jnp.zeros((META, width - 8 * tokens), F32))
    a_out[GROUP : GROUP + META] = jnp.concatenate(meta, axis=1).astype(BF16)


def select(who, step, a, b, tokens):
    width = a[0].shape[1]
    return pl.pallas_call(
        functools.partial(select_kernel, tokens, step),
        out_shape=(
            jax.ShapeDtypeStruct((GROUP + META, width), BF16),
            jax.ShapeDtypeStruct((GROUP, width), BF16),
        ),
        in_specs=[SMEM] + [VMEM] * 10,
        out_specs=(VMEM, VMEM),
        compiler_params=params(24),
        cost_estimate=cost(4 * GROUP * tokens * width, 7_000_000),
    )(who, *a, *b)


def ready_kernel(tokens, who_ref, a_ref, b_ref, wg, wu, wdt, pg, pu, db, gate, slot_out):
    me = as_float(who_ref[0])
    ids, value = [], []
    for near in range(SIDE):
        left = 2 * tokens * near
        block = a_ref[GROUP : GROUP + META, left : left + 2 * tokens].astype(F32)
        ids.append(block[:, 0:tokens])
        hit = block[:, 0:tokens] == me
        value.append(
            jnp.sum(jnp.where(hit, block[:, tokens : 2 * tokens], 0.0), axis=0, keepdims=True)
        )
    slot = slots(ids, [me] * SIDE)
    columns = [
        jnp.sum(one_hot(s, CAP) * v, axis=1, keepdims=True) for s, v in zip(slot, value)
    ]
    gate[...] = jnp.broadcast_to(jnp.concatenate(columns, axis=0), gate.shape)
    slot_out[...] = jnp.concatenate(slot + [jnp.zeros((8 - SIDE, tokens), F32)], axis=0)
    for left in range(0, pg.shape[1], 256):
        cols = slice(left, left + 256)
        rows = a_ref[0:GROUP]
        pg[:, cols] = jnp.dot(rows, wg[:, cols], preferred_element_type=F32)
        pu[:, cols] = jnp.dot(rows, wu[:, cols], preferred_element_type=F32)
        db[:, cols] = jnp.dot(b_ref[...], wdt[:, cols], preferred_element_type=F32)


def ready(who, a, b, wg, wu, wdt, tokens):
    width, hidden = wg.shape
    wide = jax.ShapeDtypeStruct((GROUP, hidden), F32)
    return pl.pallas_call(
        functools.partial(ready_kernel, tokens),
        out_shape=(
            wide,
            wide,
            wide,
            jax.ShapeDtypeStruct((GROUP, 128), F32),
            jax.ShapeDtypeStruct((8, tokens), F32),
        ),
        in_specs=[SMEM] + [VMEM] * 5,
        out_specs=[VMEM] * 5,
        compiler_params=params(8),
        cost_estimate=cost(6 * GROUP * width * hidden, 6_000_000),
    )(who, a, b, wg, wu, wdt)


def middle_kernel(tokens, *refs):
    pgs, pus, dbs, gates, slot_refs = (refs[4 * i : 4 * i + 4] for i in range(5))
    wgt, wut = refs[20:22]
    gg_out, gu_out, hg_out = refs[22:25]
    first_out, second_out = refs[25:29], refs[29:33]
    gg, gu, hg, back, slot_sum = refs[33:]
    half = first_out[0].shape[1]
    hidden_units = gg.shape[1]
    for k in range(SIDE):
        lines = []
        for near in range(SIDE):
            here = slice(near * CAP, (near + 1) * CAP)
            there = slice(k * CAP, (k + 1) * CAP)
            total = jnp.zeros((CAP, 1), F32)
            weight = gates[k][here, 0:1]
            for left in range(0, hidden_units, 256):
                cols = slice(left, left + 256)
                pre_gate, pre_up = pgs[k][here, cols], pus[k][here, cols]
                down_back = dbs[near][there, cols]
                sig = jax.nn.sigmoid(pre_gate)
                active = pre_gate * sig
                hidden = active * pre_up
                total += jnp.sum(hidden * down_back, axis=1, keepdims=True)
                scaled = weight * down_back
                gg[here, cols] = scaled * pre_up * sig * (1.0 + pre_gate * (1.0 - sig))
                gu[here, cols] = scaled * active
                row = near * GROUP + k * CAP
                hg[row : row + CAP, cols] = weight * hidden
            slot = slot_refs[k][near : near + 1]
            value = total.astype(BF16).astype(F32)
            lines.append(jnp.sum(one_hot(slot, CAP) * value, axis=0, keepdims=True))
        at = slice(k * GROUP, (k + 1) * GROUP)
        grad_gate, grad_up = gg[...].astype(BF16), gu[...].astype(BF16)
        gg_out[at] = grad_gate
        gu_out[at] = grad_up
        for left in range(0, 2 * half, 512):
            cols = slice(left, left + 512)
            rows = jnp.dot(grad_gate, wgt[:, cols], preferred_element_type=F32) + jnp.dot(
                grad_up, wut[:, cols], preferred_element_type=F32
            )
            if left < half:
                first_out[k][0:GROUP, cols] = rows.astype(BF16)
            else:
                back[at, left - half : left - half + 512] = rows
        lines.append(jnp.zeros((META - SIDE, tokens), F32))
        table = jnp.concatenate(lines, axis=0)
        table = jnp.concatenate([table, jnp.zeros((META, half - tokens), F32)], axis=1)
        first_out[k][GROUP : GROUP + META] = table.astype(BF16)
    for near in range(SIDE):
        rows = [back[k * GROUP + near * CAP : k * GROUP + (near + 1) * CAP] for k in range(SIDE)]
        second_out[near][...] = jnp.concatenate(rows, axis=0).astype(BF16)
    hg_out[...] = hg[...].astype(BF16)


def middle(pg, pu, db, gate, slot, wgt, wut, tokens):
    hidden, width = wgt.shape
    rows, half = SIDE * GROUP, width // 2
    return pl.pallas_call(
        functools.partial(middle_kernel, tokens),
        out_shape=(
            [jax.ShapeDtypeStruct((rows, hidden), BF16)] * 3
            + [jax.ShapeDtypeStruct((GROUP + META, half), BF16)] * SIDE
            + [jax.ShapeDtypeStruct((GROUP, half), BF16)] * SIDE
        ),
        in_specs=[VMEM] * 22,
        out_specs=[VMEM] * 11,
        scratch_shapes=[
            pltpu.VMEM((GROUP, hidden), F32),
            pltpu.VMEM((GROUP, hidden), F32),
            pltpu.VMEM((rows, hidden), F32),
            pltpu.VMEM((rows, half), F32),
            pltpu.VMEM((rows, 1), F32),
        ],
        compiler_params=params(14),
        cost_estimate=cost(4 * rows * width * hidden, 10_000_000),
    )(*pg, *pu, *db, *gate, *slot, wgt, wut)


def up_wgrad_kernel(*refs):
    a_refs, (gg, gu), (gate_out, up_out) = refs[:4], refs[4:6], refs[6:]
    a = jnp.concatenate([r[0:GROUP] for r in a_refs], axis=0)
    gate_out[...] = lax.dot_general(a, gg[...], BY_ROWS, preferred_element_type=F32).astype(BF16)
    up_out[...] = lax.dot_general(a, gu[...], BY_ROWS, preferred_element_type=F32).astype(BF16)


def up_wgrads(a, gg, gu):
    rows, hidden = gg.shape
    width = a[0].shape[1]
    tile = 256
    whole = pl.BlockSpec((rows, hidden), lambda d: (0, 0), pipeline_mode=pl.Buffered(1))
    return pl.pallas_call(
        up_wgrad_kernel,
        grid=(width // tile,),
        out_shape=[jax.ShapeDtypeStruct((width, hidden), BF16)] * 2,
        in_specs=[pl.BlockSpec((GROUP + META, tile), lambda d: (0, d))] * SIDE + [whole] * 2,
        out_specs=[pl.BlockSpec((tile, hidden), lambda d: (d, 0))] * 2,
        compiler_params=params(20),
        cost_estimate=cost(4 * rows * width * hidden, 15_000_000),
    )(*a, gg, gu)


def down_wgrad_kernel(*refs):
    b_refs, (hg, down_out) = refs[:4], refs[4:]
    b = jnp.concatenate([r[...] for r in b_refs], axis=0)
    down_out[...] = lax.dot_general(hg[...], b, BY_ROWS, preferred_element_type=F32).astype(BF16)


def down_wgrads(b, hg):
    rows, hidden = hg.shape
    width = b[0].shape[1]
    tile = 512
    return pl.pallas_call(
        down_wgrad_kernel,
        grid=(width // tile,),
        out_shape=jax.ShapeDtypeStruct((hidden, width), BF16),
        in_specs=[pl.BlockSpec((GROUP, tile), lambda d: (0, d))] * SIDE
        + [pl.BlockSpec((rows, hidden), lambda d: (0, 0), pipeline_mode=pl.Buffered(1))],
        out_specs=pl.BlockSpec((hidden, tile), lambda d: (0, d)),
        compiler_params=params(20),
        cost_estimate=cost(2 * rows * width * hidden, 10_000_000),
    )(*b, hg)


def places_kernel(tokens, along_row, who_ref, *refs):
    id_refs, out = refs[:4], refs[4]
    ids = [meta_of(r, tokens) for r in id_refs]
    pairs = [(near, far) for near in range(SIDE) for far in range(SIDE)]
    me = who_ref[0]
    experts = [as_float(ahead(me, 0, f) if along_row else ahead(me, f, 0)) for f in range(SIDE)]
    slot = slots([ids[n] for n, _ in pairs], [experts[f] for _, f in pairs])
    for near in range(SIDE):
        spread = [one_hot(slot[near * SIDE + far], GROUP, near * CAP) for far in range(SIDE)]
        out[near * tokens : (near + 1) * tokens] = jnp.concatenate(spread, axis=0).T.astype(BF16)


def places(who, blocks, tokens, along_row):
    return pl.pallas_call(
        functools.partial(places_kernel, tokens, along_row),
        out_shape=jax.ShapeDtypeStruct((SIDE * tokens, SIDE * GROUP), BF16),
        in_specs=[SMEM] + [VMEM] * 4,
        out_specs=VMEM,
        compiler_params=params(6),
        cost_estimate=cost(0, 4_000_000),
    )(who, *with_meta(blocks))


def gather_kernel(tokens, along_row, places_ref, *refs):
    back_refs, outs = refs[:4], refs[4:]
    half = back_refs[0].shape[1]
    for left in range(0, half, 512):
        cols = slice(left, left + 512)
        rows = jnp.concatenate([r[0:GROUP, cols] for r in back_refs], axis=0)
        for near in range(SIDE):
            mine = places_ref[near * tokens : (near + 1) * tokens]
            part = jnp.dot(mine, rows, preferred_element_type=F32)
            outs[near][0:tokens, cols] = part.astype(BF16)
    if along_row:
        tables = [r[GROUP : GROUP + META, 0:tokens].astype(F32) for r in back_refs]
        for near in range(SIDE):
            lines = [t[near : near + 1] for t in tables]
            lines.append(jnp.zeros((META - SIDE, tokens), F32))
            table = jnp.concatenate(lines, axis=0)
            table = jnp.concatenate([table, jnp.zeros((META, half - tokens), F32)], axis=1)
            outs[near][tokens : tokens + META] = table.astype(BF16)


def gather(spots, back, tokens, along_row):
    half = back[0].shape[1]
    rows = tokens + META if along_row else tokens
    return pl.pallas_call(
        functools.partial(gather_kernel, tokens, along_row),
        out_shape=[jax.ShapeDtypeStruct((rows, half), BF16)] * SIDE,
        in_specs=[VMEM] * 5,
        out_specs=[VMEM] * SIDE,
        compiler_params=params(8),
        cost_estimate=cost(32 * tokens * GROUP * half, 6_000_000),
    )(spots, *back)


def summed(tokens, g, parts):
    moe = parts[0][0:tokens].astype(F32)
    for part in parts[1:]:
        moe += part[0:tokens].astype(F32)
    moe = moe.astype(BF16).astype(F32)
    return (g.astype(F32) + moe).astype(BF16)


def finish_first_kernel(tokens, who_ref, g_ref, ids_ref, *refs):
    parts, (out, gate_out) = refs[:4], refs[4:]
    out[...] = summed(tokens, g_ref[:, 0 : out.shape[1]], parts)
    ids, me = ids_ref[...], who_ref[0]
    grad = jnp.zeros(ids.shape, F32)
    for near in range(SIDE):
        table = parts[near][tokens : tokens + META, 0:tokens].astype(F32)
        for far in range(SIDE):
            grad += jnp.where(ids == ahead(me, near, far), table[far : far + 1], 0.0)
    gate_out[...] = grad.astype(BF16)


def finish_first(who, g, ids, parts):
    tokens = g.shape[0]
    return pl.pallas_call(
        functools.partial(finish_first_kernel, tokens),
        out_shape=(
            jax.ShapeDtypeStruct((tokens, parts[0].shape[1]), BF16),
            jax.ShapeDtypeStruct(ids.shape, BF16),
        ),
        in_specs=[SMEM] + [VMEM] * 6,
        out_specs=(VMEM, VMEM),
        compiler_params=params(4),
        cost_estimate=cost(0, 2_000_000),
    )(who, g, ids, *parts)


def finish_second_kernel(tokens, g_ref, *refs):
    parts, out = refs[:4], refs[4]
    half = out.shape[1]
    out[...] = summed(tokens, g_ref[:, half : 2 * half], parts)


def finish_second(g, parts):
    tokens = g.shape[0]
    return pl.pallas_call(
        functools.partial(finish_second_kernel, tokens),
        out_shape=jax.ShapeDtypeStruct((tokens, parts[0].shape[1]), BF16),
        in_specs=[VMEM] * 5,
        out_specs=VMEM,
        compiler_params=params(4),
        cost_estimate=cost(0, 2_000_000),
    )(g, *parts)


def exchange(one, two, one_route, two_route, rounds, meanwhile=lambda: ()):
    one, two = list(one), list(two)
    for d in (1, 3):
        one[d] = shift(one[d], *one_route(d))
        two[d] = shift(two[d], *two_route(d))
    done = meanwhile()
    if rounds:
        near = (one[1], one[3], two[1], two[3])
        one[2], two[2] = after(one[2], *near, *done), after(two[2], *near, *done)
    else:
        two[2] = after(two[2], two[1], *done)
    one[2], two[2] = shift(one[2], *one_route(2)), shift(two[2], *two_route(2))
    return one, two


def local(inputs, out_grad, expert_ids, gate_probs, gate_weight, up_weight, down_weight):
    x, g = inputs[0], out_grad[0]
    tokens = x.shape[0]
    ids, gates = expert_ids[0].T, gate_probs[0].T
    who = lax.axis_index("expert").astype(jnp.int32)[None]

    a0, b0 = pack(x, g, ids, gates)
    wg, wu, wd = gate_weight[0, 0], up_weight[0, 0], down_weight[0, 0]
    wdt, wut = turned(after(wd, a0)), turned(after(wu, a0))
    a1, b1, a3, b3 = shift(a0, 1, 0), shift(b0, 0, 1), shift(a0, 3, 0), shift(b0, 0, 3)
    half = tokens // 2
    a_low, b_low, a_high, b_high = pieces((after(a1, wdt), b1), (a3, b3), half)
    a_low, b_low = shift(a_low, 1, 0), shift(b_low, 0, 1)
    a_high, b_high = shift(a_high, 3, 0), shift(b_high, 0, 3)
    a, b = (a0, a1, a_low, a_high, a3), (b0, b1, b_low, b_high, b3)
    wgt = turned(after(wg, wut))

    send_a, send_b, turn = [None] * SIDE, [None] * SIDE, after(who, wgt)
    for d in (1, 3, 2, 0):
        send_a[d], send_b[d] = select(turn, d, a, b, tokens)
        turn = after(who, send_a[d])
    own = ready(who, send_a[0], send_b[0], wg, wu, wdt, tokens)
    row_spots = places(after(who, own[-1]), a, tokens, True)
    col_spots = places(after(who, row_spots), b, tokens, False)
    rows_in, rows_grad = exchange(
        send_a, send_b, lambda d: (0, d), lambda d: (d, 0), True, lambda: (own[-1], col_spots)
    )

    made = [own]
    for d in (1, 2, 3):
        made.append(ready(who, rows_in[d], rows_grad[d], wg, wu, wdt, tokens))
    made = middle(*zip(*made), wgt, wut, tokens)
    gg, gu, hg = made[:3]
    down_wgrad = down_wgrads(rows_grad, hg)
    first, second = exchange(
        made[3:7], made[7:11], lambda d: (0, -d), lambda d: (-d, 0), False, lambda: (down_wgrad,)
    )
    gate_wgrad, up_wgrad = up_wgrads(rows_in, gg, gu)

    first = gather(after(row_spots, gate_wgrad), first, tokens, True)
    second = gather(after(col_spots, gate_wgrad), second, tokens, False)
    first, second = exchange(first, second, lambda d: (-d, 0), lambda d: (0, -d), False)
    sections = lax.axis_size("section")
    back_one = [(i + 1, i) for i in range(sections - 1)]
    handed_second = lax.ppermute(finish_second(g, second), "section", back_one)
    grad_first, gate_grad = finish_first(who, g, ids, first)
    handed_first = lax.ppermute(grad_first, "section", back_one)
    handed = jnp.concatenate([handed_first, handed_second], axis=1)
    return (
        handed[None],
        gate_grad.T[None],
        gate_wgrad[None, None],
        up_wgrad[None, None],
        down_wgrad[None, None],
    )


def solution(mesh):
    rows, mats = P("section", "expert", None), P("section", "expert", None, None)
    return jax.shard_map(
        local,
        mesh=mesh,
        in_specs=(rows, rows, rows, rows, mats, mats, mats),
        out_specs=(rows, rows, mats, mats, mats),
        check_vma=False,
    )
```
